32 devices in a mesh: rep: 2 (over y), fsdp: 4 (over x, core), ctx: 4 (over z).
Axes of the slice: x: 2, y: 2, z: 4, core: 2. Of those that a mesh axis runs over, the one named last changes fastest.
Arguments:
- patches: bfloat16 [8, 640, 1152], P(('rep', 'fsdp'), 'ctx'), may hold values from -6 to 6
- picture: int32 [8, 640], P(('rep', 'fsdp')), may hold values from 0 to 3, as said below
- gain_one: bfloat16 [1152], P('fsdp'), may hold values from 0.5 to 1.5
- shift_one: bfloat16 [1152], P('fsdp'), may hold values from -1.75 to 1.75
- qkv_weight: bfloat16 [1152, 3456], P('fsdp'), may hold values from -0.1875 to 0.1875
- query_bias: bfloat16 [1152], P('fsdp'), may hold values from -1.75 to 1.75
- value_bias: bfloat16 [1152], P('fsdp'), may hold values from -1.75 to 1.75
- out_weight: bfloat16 [1152, 1152], P('fsdp'), may hold values from -0.5 to 0.5
- out_bias: bfloat16 [1152], P('fsdp'), may hold values from -1.75 to 1.75
- gain_two: bfloat16 [1152], P('fsdp'), may hold values from 0.5 to 1.5
- shift_two: bfloat16 [1152], P('fsdp'), may hold values from -1.75 to 1.75
- up_weight: bfloat16 [1152, 4304], P('fsdp'), may hold values from -0.1875 to 0.1875
- up_bias: bfloat16 [4304], P('fsdp'), may hold values from -1.75 to 1.75
- down_weight: bfloat16 [4304, 1152], P('fsdp'), may hold values from -0.09375 to 0.09375
- down_bias: bfloat16 [1152], P('fsdp'), may hold values from -1.75 to 1.75
- cotangent: bfloat16 [8, 640, 1152], P(('rep', 'fsdp'), 'ctx'), may hold values from -6 to 6
Outputs:
- output: bfloat16 [8, 640, 1152], P(('rep', 'fsdp'), 'ctx')
- input_grad: bfloat16 [8, 640, 1152], P(('rep', 'fsdp'), 'ctx')
- gain_one_grad: float32 [1152], P('fsdp')
- shift_one_grad: float32 [1152], P('fsdp')
- qkv_weight_grad: float32 [1152, 3456], P('fsdp')
- query_bias_grad: float32 [1152], P('fsdp')
- value_bias_grad: float32 [1152], P('fsdp')
- out_weight_grad: float32 [1152, 1152], P('fsdp')
- out_bias_grad: float32 [1152], P('fsdp')
- gain_two_grad: float32 [1152], P('fsdp')
- shift_two_grad: float32 [1152], P('fsdp')
- up_weight_grad: float32 [1152, 4304], P('fsdp')
- up_bias_grad: float32 [4304], P('fsdp')
- down_weight_grad: float32 [4304, 1152], P('fsdp')
- down_bias_grad: float32 [1152], P('fsdp')
The draws below stay inside these ranges and needn't reach their ends.
Inputs may be any that keep to these rules, and one draw needn't show every extreme that they name: Along each row the values never fall; 0 to 2 are pictures, each present, and 3 marks padding at the row's end; one picture of each row, which one drawn from the seed, holds all but at most 3 * max(40, 1) tokens; every other picture and the padding hold 1 to max(40, 1) tokens.
All inputs are finite; a program needn't handle non-finite values.
Results may differ from the reference program's by a relative error of at most 0.019.
Values may be sent and summed in bfloat16 or wider, within the bound.
No kernel may reach another device: no remote copies, remote signals or barrier semaphores. Data moves between devices by JAX's collectives and lax.ppermute only.
A program may use at most 256 MiB of HBM per device.

```python
import jax
import jax.numpy as jnp
from jax import lax

D = 1152
HEADS = 16
HEAD_DIM = 72
FF = 4304
SEG = 160
PICS = 3
LEN = 640
ROWS = 8


def draw_picture(key, part):
    key = jax.random.fold_in(key, 7)
    key_lens, key_pick = jax.random.split(key)
    piece_cap = max(SEG // 4, 1)
    piece_lens = jax.random.randint(key_lens, (ROWS, PICS + 1), 1, piece_cap + 1)
    chosen = jax.random.randint(key_pick, (ROWS, 1), 0, PICS)
    columns = jnp.arange(PICS + 1, dtype=jnp.int32)[None, :]
    others = jnp.sum(jnp.where(columns == chosen, 0, piece_lens), axis=1, keepdims=True)
    lengths_all = jnp.where(columns == chosen, LEN - others, piece_lens)
    bounds = jnp.cumsum(lengths_all, axis=1)
    positions = jnp.arange(LEN, dtype=jnp.int32)
    return jnp.sum((positions[None, :, None] >= bounds[:, None, :]).astype(jnp.int32), axis=2)


def level_of(own_key, shape, cuts, low, high):
    def one(position, shards_of):
        heights = jax.random.uniform(jax.random.fold_in(jax.random.fold_in(own_key, 6), position), (shards_of,), jnp.float32, low / len(cuts), high / len(cuts))
        return jnp.repeat(jnp.exp(heights), shape[position] // shards_of).reshape((-1,) + (1,) * (len(shape) - position - 1))

    factor_of = one(*cuts[0])
    for cut in cuts[1:]:
        factor_of = factor_of * one(*cut)
    return factor_of


def noise(stream_key, extent, scale, bound, cuts=(), held_as=jnp.bfloat16):
    values = jax.random.normal(stream_key, extent, jnp.float32) * scale
    if len(cuts) > 0:
        values = level_of(stream_key, extent, cuts, -0.22, 0.18) * values
    return jnp.clip(values, min=-bound, max=bound).astype(held_as)


def setup_inputs(seed: int = 0) -> dict:
    splits = jax.random.split(jax.random.key(seed), 17)
    return {
        "patches": noise(splits[0], (ROWS, LEN, D), 1.0, 6.0, ((0, 8), (1, 4))),
        "picture": draw_picture(jax.random.fold_in(splits[16], 71), 0),
        "gain_one": jnp.clip(1.0 + 0.1 * jax.random.normal(splits[2], (D,), jnp.float32), 0.5, 1.5).astype(jnp.bfloat16),
        "shift_one": noise(splits[3], (D,), 0.3, 1.75, ((0, 4),)),
        "qkv_weight": noise(splits[4], (D, 3 * D), D ** -0.5, 0.1875, ((0, 4),)),
        "query_bias": noise(splits[5], (D,), 0.3, 1.75, ((0, 4),)),
        "value_bias": noise(splits[6], (D,), 0.3, 1.75, ((0, 4),)),
        "out_weight": noise(splits[7], (D, D), (D // 8) ** -0.5, 0.5, ((0, 4),)),
        "out_bias": noise(splits[8], (D,), 0.3, 1.75, ((0, 4),)),
        "gain_two": jnp.clip(1.0 + 0.1 * jax.random.normal(splits[9], (D,), jnp.float32), 0.5, 1.5).astype(jnp.bfloat16),
        "shift_two": noise(splits[10], (D,), 0.3, 1.75, ((0, 4),)),
        "up_weight": noise(splits[11], (D, FF), D ** -0.5, 0.1875, ((0, 4),)),
        "up_bias": noise(splits[12], (FF,), 0.3, 1.75, ((0, 4),)),
        "down_weight": noise(splits[13], (FF, D), FF ** -0.5, 0.09375, ((0, 4),)),
        "down_bias": noise(splits[14], (D,), 0.3, 1.75, ((0, 4),)),
        "cotangent": noise(splits[15], (ROWS, LEN, D), 1.0, 6.0, ((0, 8), (1, 4))),
    }


EPSILON = 1e-06
MASKED = -1e+30

@jax.custom_vjp
def low(v):
    return lax.optimization_barrier(v.astype(jnp.bfloat16)).astype(jnp.float32)

@jax.custom_vjp
def low_back(v):
    return v

def low_keep(v):
    return (low(v), None)

def low_pass(kept, grad):
    return (grad,)

def back_keep(v):
    return (v, None)

def back_low(kept, grad):
    return (low(grad),)
low.defvjp(low_keep, low_pass)
low_back.defvjp(back_keep, back_low)

def layer_norm(values, gain_vec, shift_vec):
    center = values - lax.optimization_barrier(jnp.mean(values, axis=-1, keepdims=True))
    spread = lax.optimization_barrier(jnp.mean(center * center, axis=-1, keepdims=True))
    return center * lax.rsqrt(spread + EPSILON) * gain_vec + shift_vec

def matmul(left, right):
    return jnp.dot(left, right, precision=lax.Precision.HIGHEST)

def encoder_layer(params, row_tokens, row_picture):
    gain_first, shift_first, qkv_full, query_shift, value_shift, out_full, out_shift, gain_second, shift_second, up_full, up_shift, down_full, down_shift = params
    seq_len = row_tokens.shape[0]
    positions = jnp.arange(seq_len, dtype=jnp.int32)
    allowed = (row_picture[:, None] == row_picture[None, :]) & ((row_picture[None, :] != PICS) | (positions[:, None] == positions[None, :]))
    normed_one = low(layer_norm(row_tokens, gain_first, shift_first))
    projected = low_back(matmul(normed_one, qkv_full))
    queries = low(HEAD_DIM ** (-0.5) * (projected[:, :D] + query_shift))
    key_vecs = low(projected[:, D:2 * D])
    value_vecs = low(projected[:, 2 * D:] + value_shift)
    query_heads = queries.reshape(seq_len, HEADS, HEAD_DIM)
    key_heads = key_vecs.reshape(seq_len, HEADS, HEAD_DIM)
    value_heads = value_vecs.reshape(seq_len, HEADS, HEAD_DIM)
    dot_scores = jnp.einsum('qhd,khd->hqk', query_heads, key_heads, precision=lax.Precision.HIGHEST)
    scores = low_back(jnp.where(allowed[None], dot_scores, MASKED))
    probs = low(jax.nn.softmax(scores, axis=-1))
    mixed_heads = jnp.einsum('hqk,khd->qhd', probs, value_heads, precision=lax.Precision.HIGHEST)
    mixed = low(low_back(mixed_heads.reshape(seq_len, D)))
    attended = row_tokens + low_back(matmul(mixed, out_full) + out_shift)
    normed_two = low(layer_norm(attended, gain_second, shift_second))
    hidden = low_back(matmul(normed_two, up_full) + up_shift)
    activated = low(jax.nn.gelu(hidden, approximate=True))
    return attended + low_back(matmul(activated, down_full) + down_shift)

def reference(patches, picture, gain_one, shift_one, qkv_weight, query_bias, value_bias, out_weight, out_bias, gain_two, shift_two, up_weight, up_bias, down_weight, down_bias, cotangent):
    params = tuple((member.astype(jnp.float32) for member in (gain_one, shift_one, qkv_weight, query_bias, value_bias, out_weight, out_bias, gain_two, shift_two, up_weight, up_bias, down_weight, down_bias)))

    def scan_step(summed_grads, row_data):
        row_tokens, row_picture, row_cot = row_data

        def forward(param_set, token_set):
            return encoder_layer(param_set, token_set, row_picture)
        result, backward = jax.vjp(forward, params, row_tokens.astype(jnp.float32))
        param_grads, token_grads = backward(row_cot.astype(jnp.float32))
        summed_grads = jax.tree.map(jnp.add, summed_grads, param_grads)
        return (summed_grads, (result.astype(jnp.bfloat16), token_grads.astype(jnp.bfloat16)))
    zero_grads = jax.tree.map(jnp.zeros_like, params)
    grads, (outputs, input_grads) = lax.scan(scan_step, zero_grads, (patches, picture, cotangent))
    return (outputs, input_grads, grads[0], grads[1], grads[2], grads[3], grads[4], grads[5], grads[6], grads[7], grads[8], grads[9], grads[10], grads[11], grads[12])
```

```python
import functools

import jax
import jax.numpy as jnp
from jax import lax
from jax.experimental import pallas as pl
from jax.experimental.pallas import tpu as pltpu
from jax.sharding import PartitionSpec as P

HEADS = 16
HEAD_DIM = 72
PICS = 3

EPSILON = 1e-06
MASKED = -1e30
BF = jnp.bfloat16
F32 = jnp.float32
SCALING = HEAD_DIM ** (-0.5)


def dot(left, right):
    return jnp.dot(left, right, preferred_element_type=F32)


def dot_t(left, right):
    return lax.dot_general(left, right, (((1,), (1,)), ((), ())), preferred_element_type=F32)


def t_dot(left, right):
    return lax.dot_general(left, right, (((0,), (0,)), ((), ())), preferred_element_type=F32)


def norm_parts(values):
    center = values - jnp.mean(values, axis=-1, keepdims=True)
    spread = jnp.mean(center * center, axis=-1, keepdims=True)
    scale = lax.rsqrt(spread + EPSILON)
    return center * scale, scale


def norm_back(grad, normal, scale, gain):
    through = grad * gain
    mean_one = jnp.mean(through, axis=-1, keepdims=True)
    mean_two = jnp.mean(through * normal, axis=-1, keepdims=True)
    back = scale * (through - mean_one - normal * mean_two)
    return back, jnp.sum(grad * normal, axis=0), jnp.sum(grad, axis=0)


def gelu_tanh(values):
    return jax.nn.gelu(values, approximate=True)


def allowed_of(pic_col, pic_row, first):
    block, total = pic_col.shape[0], pic_row.shape[1]
    rows = lax.broadcasted_iota(jnp.int32, (block, total), 0) + first
    columns = lax.broadcasted_iota(jnp.int32, (block, total), 1)
    return (pic_col == pic_row) & ((pic_row != PICS) | (rows == columns))


def attend_kernel(heads, pic_col, pic_row, q_ref, k_ref, v_ref, mixed_ref, log_ref):
    block = q_ref.shape[0]
    allowed = allowed_of(pic_col[...], pic_row[...], pl.program_id(0) * block)
    mixed, logs = [], []
    for h in range(heads):
        cut = slice(h * HEAD_DIM, (h + 1) * HEAD_DIM)
        scores = dot_t(q_ref[:, cut], k_ref[:, cut])
        scores = jnp.where(allowed, scores, MASKED)
        largest = jnp.max(scores, axis=-1, keepdims=True)
        expo = jnp.exp(scores - largest)
        totals = jnp.sum(expo, axis=-1, keepdims=True)
        probs = (expo * (1.0 / totals)).astype(BF)
        mixed.append(dot(probs, v_ref[:, cut]))
        logs.append(largest + jnp.log(totals))
    mixed_ref[...] = jnp.concatenate(mixed, axis=1).astype(BF)
    log_ref[...] = jnp.concatenate(logs, axis=1)


def attend(pic, queries, keys, values, block):
    total, width = queries.shape
    heads = width // HEAD_DIM
    whole = pl.BlockSpec((total, width), lambda i: (0, 0))
    part = pl.BlockSpec((block, width), lambda i: (i, 0))
    return pl.pallas_call(
        functools.partial(attend_kernel, heads),
        grid=(total // block,),
        in_specs=[
            pl.BlockSpec((block, 1), lambda i: (i, 0)),
            pl.BlockSpec((1, total), lambda i: (0, 0)),
            part,
            whole,
            whole,
        ],
        out_specs=[part, pl.BlockSpec((block, heads), lambda i: (i, 0))],
        out_shape=[
            jax.ShapeDtypeStruct((total, width), BF),
            jax.ShapeDtypeStruct((total, heads), F32),
        ],
        compiler_params=pltpu.CompilerParams(vmem_limit_bytes=32 * 2**20),
    )(pic[:, None], pic[None, :], queries, keys, values)


def attend_back_kernel(
    heads, pic_col, pic_row, q_ref, mg_ref, log_ref, k_ref, v_ref,
    grad_q, grad_k, grad_v, sum_q, sum_v, acc_k, acc_v, acc_q,
):
    block = q_ref.shape[0]
    step, steps = pl.program_id(0), pl.num_programs(0)

    @pl.when(step == 0)
    def _():
        acc_k[...] = jnp.zeros_like(acc_k)
        acc_v[...] = jnp.zeros_like(acc_v)
        acc_q[...] = jnp.zeros_like(acc_q)

    allowed = allowed_of(pic_col[...], pic_row[...], step * block)
    query_parts, key_parts, value_parts = [], [], []
    for h in range(heads):
        cut = slice(h * HEAD_DIM, (h + 1) * HEAD_DIM)
        query, key, value, mixed_grad = q_ref[:, cut], k_ref[:, cut], v_ref[:, cut], mg_ref[:, cut]
        scores = jnp.where(allowed, dot_t(query, key), MASKED)
        probs = jnp.exp(scores - log_ref[:, h : h + 1])
        probs_grad = dot_t(mixed_grad, value)
        delta = jnp.sum(probs * probs_grad, axis=-1, keepdims=True)
        scores_grad = (probs * (probs_grad - delta)).astype(BF)
        query_parts.append(dot(scores_grad, key))
        key_parts.append(t_dot(scores_grad, query))
        value_parts.append(t_dot(probs.astype(BF), mixed_grad))
    query_grad = SCALING * jnp.concatenate(query_parts, axis=1)
    grad_q[...] = query_grad.astype(BF)
    acc_q[...] += jnp.sum(query_grad, axis=0, keepdims=True)
    acc_k[...] += jnp.concatenate(key_parts, axis=1)
    acc_v[...] += jnp.concatenate(value_parts, axis=1)

    @pl.when(step == steps - 1)
    def _():
        grad_k[...] = acc_k[...].astype(BF)
        grad_v[...] = acc_v[...].astype(BF)
        sum_q[...] = acc_q[...]
        sum_v[...] = jnp.sum(acc_v[...], axis=0, keepdims=True)


def attend_back(pic, queries, mixed_grad, logs, keys, values, block):
    total, width = queries.shape
    heads = width // HEAD_DIM
    whole = pl.BlockSpec((total, width), lambda i: (0, 0))
    part = pl.BlockSpec((block, width), lambda i: (i, 0))
    line = pl.BlockSpec((1, width), lambda i: (0, 0))
    low = jax.ShapeDtypeStruct((total, width), BF)
    sums = jax.ShapeDtypeStruct((1, width), F32)
    return pl.pallas_call(
        functools.partial(attend_back_kernel, heads),
        grid=(total // block,),
        in_specs=[
            pl.BlockSpec((block, 1), lambda i: (i, 0)),
            pl.BlockSpec((1, total), lambda i: (0, 0)),
            part,
            part,
            pl.BlockSpec((block, heads), lambda i: (i, 0)),
            whole,
            whole,
        ],
        out_specs=[part, whole, whole, line, line],
        out_shape=[low, low, low, sums, sums],
        scratch_shapes=[
            pltpu.VMEM((total, width), F32),
            pltpu.VMEM((total, width), F32),
            pltpu.VMEM((1, width), F32),
        ],
        compiler_params=pltpu.CompilerParams(vmem_limit_bytes=32 * 2**20),
    )(pic[:, None], pic[None, :], queries, mixed_grad, logs, keys, values)


def per_device(
    sizes,
    patches,
    picture,
    gain_one,
    shift_one,
    qkv_weight,
    query_bias,
    value_bias,
    out_weight,
    out_bias,
    gain_two,
    shift_two,
    up_weight,
    up_bias,
    down_weight,
    down_bias,
    cotangent,
):
    reps, shards, parts = sizes
    rep = lax.axis_index("rep")
    own = lax.axis_index("fsdp")
    seg, width = patches.shape[1], patches.shape[2]
    rows = width // shards
    units = up_bias.shape[0]
    order = (0, 2, 1, 3)

    def swap(value, axis, bit):
        size = {"rep": reps, "fsdp": shards, "ctx": parts}[axis]
        return lax.ppermute(value, axis, [(i, i ^ bit) for i in range(size)])

    def turn(value):
        pairs = [(f * parts + c, c * parts + f) for f in range(shards) for c in range(parts)]
        return lax.ppermute(value, ("fsdp", "ctx"), pairs)

    def gather(value):
        two = jnp.concatenate([value, swap(value, "fsdp", 2)], axis=0)
        return jnp.concatenate([two, swap(two, "fsdp", 1)], axis=0)

    def scatter(value):
        half = value.shape[0] // 2
        value = value[:half] + swap(value[half:].astype(BF), "fsdp", 1).astype(F32)
        half = half // 2
        return value[:half] + swap(value[half:].astype(BF), "fsdp", 2).astype(F32)

    def in_order_of(value, bit):
        blocks = [value[i * seg : (i + 1) * seg] for i in range(shards)]
        return jnp.concatenate([blocks[order.index(member ^ bit)] for member in order], axis=0)

    def pick(stack, index):
        return lax.dynamic_index_in_dim(stack, index, 0, keepdims=False)

    def to_columns(stack):
        half = stack.shape[1] // 2
        low = lax.rem(rep, 2)
        first = [pick(stack, own ^ bit) for bit in range(shards)]
        mine = [lax.dynamic_slice_in_dim(first[bit], low * half, half) for bit in (2, 3)]
        across = jnp.stack([swap(mine[0], "fsdp", 2), swap(mine[1], "fsdp", 3)])
        other = swap(across, "rep", 1)
        lower = jnp.where(low == 0, across, other)
        upper = jnp.where(low == 0, other, across)
        far = jnp.concatenate([lower, upper], axis=1)
        near = jnp.stack([first[0], swap(first[1], "fsdp", 1)])
        blocks = jnp.concatenate([near, far], axis=0)
        return jnp.concatenate([pick(blocks, own ^ f) for f in range(shards)], axis=0)

    tokens = gather(turn(patches[0]))
    row_picture = turn(picture[0])
    pic = jnp.concatenate([lax.dynamic_slice_in_dim(row_picture, (own ^ bit) * seg, seg) for bit in order])

    vectors = lax.all_gather(
        jnp.stack([gain_one, shift_one, gain_two, shift_two, out_bias, down_bias]), "fsdp", axis=1, tiled=True
    ).astype(F32)
    gain_first, shift_first, gain_second, shift_second, out_shift, down_shift = [vectors[i] for i in range(6)]

    qkv_own = to_columns(
        jnp.stack(
            [
                jnp.concatenate(
                    [qkv_weight[:, s * width + f * rows : s * width + (f + 1) * rows] for s in range(3)], axis=1
                )
                for f in range(shards)
            ]
        )
    )
    up_own = to_columns(jnp.stack([up_weight[:, f * units : (f + 1) * units] for f in range(shards)]))
    out_full = gather(out_weight)
    cot_own = turn(cotangent[0])
    cot = gather(cot_own)

    inputs = tokens.astype(F32)
    normal_one, scale_one = norm_parts(inputs)
    normed_one = (normal_one * gain_first + shift_first).astype(BF)
    projected = dot(normed_one, qkv_own)
    queries = (SCALING * (projected[:, :rows] + query_bias.astype(F32))).astype(BF)
    keys = projected[:, rows : 2 * rows].astype(BF)
    values = (projected[:, 2 * rows :] + value_bias.astype(F32)).astype(BF)
    mixed, logs = attend(pic, queries, keys, values, seg)
    mixed_two = swap(in_order_of(mixed, 2), "fsdp", 2)
    mixed_one = swap(in_order_of(mixed, 1), "fsdp", 1)
    mixed_three = swap(in_order_of(mixed_two, 1), "fsdp", 1)
    branch = (
        dot(mixed, out_full[:rows])
        + dot(mixed_two, out_full[rows : 2 * rows])
        + dot(mixed_one, out_full[2 * rows : 3 * rows])
        + dot(mixed_three, out_full[3 * rows :])
    )
    attended = inputs + branch + out_shift
    normal_two, scale_two = norm_parts(attended)
    normed_two = (normal_two * gain_second + shift_second).astype(BF)
    hidden = dot(normed_two, up_own) + up_bias.astype(F32)
    activated = gelu_tanh(hidden).astype(BF)
    summed = scatter(dot(activated, down_weight))
    output = turn((attended[:seg] + summed + down_shift).astype(BF))

    down_weight_grad = t_dot(activated, cot)
    act_grad = dot_t(cot, down_weight)
    hidden_grad = jax.vjp(gelu_tanh, hidden)[1](act_grad)[0].astype(BF)
    up_weight_grad = t_dot(normed_two, hidden_grad)
    normed_two_grad = scatter(dot_t(hidden_grad, up_own))
    back_two, gain_two_grad, shift_two_grad = norm_back(
        normed_two_grad, normal_two[:seg], scale_two[:seg], gain_second
    )
    attended_grad = cot_own.astype(F32) + back_two
    branch_grad = gather(attended_grad.astype(BF))
    out_weight_grad = t_dot(mixed, branch_grad)
    mixed_grad = dot_t(branch_grad, out_weight).astype(BF)
    query_grad, key_grad, value_grad, query_sum, value_sum = attend_back(
        pic, queries, mixed_grad, logs, keys, values, seg
    )
    projected_grad = jnp.concatenate([query_grad, key_grad, value_grad], axis=1)
    qkv_weight_grad = t_dot(normed_one, projected_grad)
    normed_one_grad = scatter(dot_t(projected_grad, qkv_own))
    back_one, gain_one_grad, shift_one_grad = norm_back(
        normed_one_grad, normal_one[:seg], scale_one[:seg], gain_first
    )
    input_grad = turn((attended_grad + back_one).astype(BF))

    def reduce_groups(value, first, second):
        kept = []
        for axis in (first, second):
            low = lax.rem(lax.axis_index(axis), 2)
            half = value.shape[1] // 2
            send = lax.dynamic_slice_in_dim(value, (1 - low) * half, half, 1).astype(BF)
            value = lax.dynamic_slice_in_dim(value, low * half, half, 1).astype(F32) + swap(send, axis, 1).astype(F32)
            kept.append(low)
        bit = 2
        while bit < parts:
            value = value.astype(BF).astype(F32) + swap(value.astype(BF), "ctx", bit).astype(F32)
            bit *= 2
        bit = 2
        while bit < reps:
            value = value.astype(BF).astype(F32) + swap(value.astype(BF), "rep", bit).astype(F32)
            bit *= 2
        return value.astype(BF), kept

    def spread(value, kept, first, second):
        for axis, low in ((second, kept[1]), (first, kept[0])):
            other = swap(value, axis, 1)
            value = jnp.concatenate([jnp.where(low == 0, value, other), jnp.where(low == 0, other, value)], axis=-2)
        return value

    def total_rows(value, first, second):
        value, kept = reduce_groups(value[None], first, second)
        return spread(value[0], kept, first, second)

    def total_columns(value, first, second):
        value, kept = reduce_groups(value.reshape((shards, rows) + value.shape[1:]), first, second)
        blocks = [pick(value, own)] + [swap(pick(value, own ^ bit), "fsdp", bit) for bit in range(1, shards)]
        blocks = jnp.stack(blocks)
        return spread(jnp.stack([pick(blocks, own ^ f) for f in range(shards)]), kept, first, second)

    pad = -units % 64
    down_total = total_rows(jnp.pad(down_weight_grad, ((0, pad), (0, 0))), "rep", "ctx")[:units]
    up_parts = total_columns(up_weight_grad, "ctx", "rep")
    out_total = total_rows(out_weight_grad, "rep", "ctx")
    qkv_parts = total_columns(qkv_weight_grad, "rep", "ctx")
    up_total = jnp.concatenate([up_parts[f] for f in range(shards)], axis=1)
    qkv_total = jnp.concatenate(
        [qkv_parts[f][:, s * rows : (s + 1) * rows] for s in range(3) for f in range(shards)], axis=1
    )

    cut = lambda full: lax.dynamic_slice_in_dim(full, own * rows, rows)
    own_sums = jnp.concatenate(
        [
            query_sum[0],
            value_sum[0],
            cut(jnp.sum(branch_grad.astype(F32), axis=0)),
            cut(jnp.sum(cot.astype(F32), axis=0)),
            jnp.sum(hidden_grad.astype(F32), axis=0),
        ]
    )
    own_sums = lax.psum(own_sums, ("rep", "ctx"))
    token_sums = lax.psum(
        jnp.stack([gain_one_grad, shift_one_grad, gain_two_grad, shift_two_grad]), ("rep", "fsdp", "ctx")
    )
    token_sums = lax.dynamic_slice_in_dim(token_sums, own * rows, rows, 1)
    return (
        output[None],
        input_grad[None],
        token_sums[0],
        token_sums[1],
        qkv_total.astype(F32),
        own_sums[:rows],
        own_sums[rows : 2 * rows],
        out_total.astype(F32),
        own_sums[2 * rows : 3 * rows],
        token_sums[2],
        token_sums[3],
        up_total.astype(F32),
        own_sums[4 * rows :],
        down_total.astype(F32),
        own_sums[3 * rows : 4 * rows],
    )


def solution(mesh):
    sizes = tuple(mesh.shape[axis] for axis in ("rep", "fsdp", "ctx"))
    tokens = P(("rep", "fsdp"), "ctx", None)
    vector, matrix = P("fsdp"), P("fsdp", None)
    return jax.shard_map(
        functools.partial(per_device, sizes),
        mesh=mesh,
        in_specs=(
            tokens,
            P(("rep", "fsdp"), None),
            vector,
            vector,
            matrix,
            vector,
            vector,
            matrix,
            vector,
            vector,
            vector,
            matrix,
            vector,
            matrix,
            vector,
            tokens,
        ),
        out_specs=(
            tokens,
            tokens,
            vector,
            vector,
            matrix,
            vector,
            vector,
            matrix,
            vector,
            vector,
            vector,
            matrix,
            vector,
            matrix,
            vector,
        ),
        check_vma=False,
    )
```

```python
import functools

import jax
import jax.numpy as jnp
from jax import lax
from jax.experimental import pallas as pl
from jax.experimental.pallas import tpu as pltpu
from jax.sharding import PartitionSpec as P

HEADS = 16
HEAD_DIM = 72
PICS = 3

EPSILON = 1e-06
MASKED = -1e30
BF = jnp.bfloat16
F32 = jnp.float32
SCALING = HEAD_DIM ** (-0.5)
TANH_SCALE = (2.0 / jnp.pi) ** 0.5
CUBIC = 0.044715
VMEM_LIMIT = 32 * 2**20
ORDER = (0, 2, 1, 3)
SCHEDULE = (
    "ugrads", "ng2", "add2", "br", "K3", "addo", "d1", "K4", "d2", "ng1", "qg", "u1", "add1", "K5", "d3",
    "u2", "d4", "q1", "q2", "u3", "place_d", "u4", "q3", "u5", "q4", "q5", "place_u", "v1", "v2", "v3",
    "fin", "back", "place_q",
)
EXTRA = 16


def dot(left, right):
    return jnp.dot(left, right, preferred_element_type=F32)


def dot_t(left, right):
    return lax.dot_general(left, right, (((1,), (1,)), ((), ())), preferred_element_type=F32)


def t_dot(left, right):
    return lax.dot_general(left, right, (((0,), (0,)), ((), ())), preferred_element_type=F32)


def rows_at(index, size):
    return pl.ds(pl.multiple_of(index * size, 8), size)


def norm_parts(values):
    center = values - jnp.mean(values, axis=-1, keepdims=True)
    spread = jnp.mean(center * center, axis=-1, keepdims=True)
    scale = lax.rsqrt(spread + EPSILON)
    return center * scale, scale


def norm_back(grad, normal, scale, gain):
    through = grad * gain
    mean_one = jnp.mean(through, axis=-1, keepdims=True)
    mean_two = jnp.mean(through * normal, axis=-1, keepdims=True)
    back = scale * (through - mean_one - normal * mean_two)
    return back, jnp.sum(grad * normal, axis=0, keepdims=True), jnp.sum(grad, axis=0, keepdims=True)


def call(kernel, outs, ins, scratch=(), name=None, after=(), us=1):
    vmem = pl.BlockSpec(memory_space=pltpu.VMEM)
    skip = len(after)

    def body(*refs):
        kernel(*refs[skip:])

    return pl.pallas_call(
        body,
        out_shape=outs,
        in_specs=[pl.BlockSpec(memory_space=pl.ANY)] * skip
        + [pl.BlockSpec(memory_space=pltpu.SMEM)]
        + [vmem] * (len(ins) - 1),
        out_specs=[vmem] * len(outs),
        scratch_shapes=list(scratch),
        compiler_params=pltpu.CompilerParams(vmem_limit_bytes=VMEM_LIMIT),
        cost_estimate=pl.CostEstimate(flops=us * 10**9, bytes_accessed=0, transcendentals=0),
        name=name,
    )(*after, *ins)


def low_like(*shape):
    return jax.ShapeDtypeStruct(shape, BF)


def full_like(*shape):
    return jax.ShapeDtypeStruct(shape, F32)


def cut_columns(spans, weight, stack):
    for f, parts in enumerate(spans):
        place = 0
        for start, stop in parts:
            stack[f, :, place : place + stop - start] = weight[:, start:stop]
            place += stop - start


def cut_kernel(spans, idx, weight, vectors, near, core, far_two, far_three, stack):
    rows = weight.shape[0]
    own, low = idx[0], idx[1]
    cut_columns(spans, weight, stack)
    for bit, out in enumerate((near, core, far_two, far_three)):
        size = out.shape[0] - EXTRA
        out[:size] = stack[own ^ bit] if size == rows else stack[own ^ bit, rows_at(low, size)]
        out[size:] = jnp.zeros((EXTRA, out.shape[1]), BF)
        out[size:, : vectors.shape[1]] = vectors[...]


def cut_both_kernel(spans, idx, weight, out_weight, near, core, far, stack):
    own, low = idx[0], idx[2]
    half = weight.shape[0] // 2
    columns = weight.shape[1] // len(spans)
    cut_columns(spans, weight, stack)
    near[...] = stack[own]
    core[0, :, :columns] = stack[own ^ 1]
    core[1] = out_weight[...]
    far[0, :, :columns] = stack[own ^ 2, rows_at(low, half)]
    far[1, :, :columns] = stack[own ^ 3, rows_at(low, half)]
    far[2] = out_weight[rows_at(low, half)]


def place_halves(low, target, block, mine, other):
    half = mine.shape[0]
    target[rows_at(2 * block + low, half)] = mine
    target[rows_at(2 * block + 1 - low, half)] = other


def join_tokens_kernel(idx, *refs):
    for i, ref in enumerate(refs[:-1]):
        for f in range(ref.shape[0]):
            refs[-1][f, i] = ref[f]


def part_tokens_kernel(idx, source, *outs):
    for i, out in enumerate(outs):
        for c in range(out.shape[0]):
            out[c] = source[c, i]


def allowed_of(pic_col, pic_row):
    total = pic_row.shape[1]
    rows = lax.broadcasted_iota(jnp.int32, (total, total), 0)
    columns = lax.broadcasted_iota(jnp.int32, (total, total), 1)
    return (pic_col == pic_row) & ((pic_row != PICS) | (rows == columns))


def project_kernel(
    idx, tok_0, tok_2, tok_1, tok_3, near, core, far_two, far_two_y, far_three, far_three_y, pic_col, pic_row, query_bias, value_bias,
    tokens, normed, weight, vectors, queries, keys, values, mixed, logs, pieces,
):
    own = idx[0]
    rows = queries.shape[1]
    block = tok_0.shape[0]
    half = rows // 2
    weight[rows_at(own, rows)] = near[:rows]
    weight[rows_at(own ^ 1, rows)] = core[:rows]
    place_halves(idx[1], weight, own ^ 2, far_two[:half], far_two_y[:half])
    place_halves(idx[1], weight, own ^ 3, far_three[:half], far_three_y[:half])
    for bit, ref in enumerate((near, core, far_two, far_three)):
        pieces[bit] = ref[ref.shape[0] - EXTRA :, :rows].astype(F32)[:8]
    vectors[...] = jnp.concatenate([pieces[own ^ f] for f in range(len(ORDER))], axis=1)
    gain, shift = vectors[0:1], vectors[1:2]
    for bit, ref in zip(ORDER, (tok_0, tok_2, tok_1, tok_3)):
        part = ref[...]
        tokens[rows_at(own ^ bit, block)] = part
        normed[rows_at(own ^ bit, block)] = (norm_parts(part.astype(F32))[0] * gain + shift).astype(BF)
    query_add, value_add = query_bias[...].astype(F32), value_bias[...].astype(F32)

    result = dot(normed[...], weight[...])
    queries[...] = (SCALING * (result[:, :rows] + query_add)).astype(BF)
    keys[...] = result[:, rows : 2 * rows].astype(BF)
    values[...] = (result[:, 2 * rows :] + value_add).astype(BF)
    allowed = allowed_of(pic_col[...], pic_row[...])
    outs, log_parts = [], []
    for h in range(rows // HEAD_DIM):
        cut = slice(h * HEAD_DIM, (h + 1) * HEAD_DIM)
        scores = jnp.where(allowed, dot_t(queries[:, cut], keys[:, cut]), MASKED)
        largest = jnp.max(scores, axis=-1, keepdims=True)
        expo = jnp.exp(scores - largest)
        sums = jnp.sum(expo, axis=-1, keepdims=True)
        probs = (expo * (1.0 / sums)).astype(BF)
        outs.append(dot(probs, values[:, cut]))
        log_parts.append(largest + jnp.log(sums))
    mixed[...] = jnp.concatenate(outs, axis=1).astype(BF)
    logs[...] = jnp.concatenate(log_parts, axis=1)


def unit_kernel(
    idx, tokens, mix_0, mix_2, mix_1, mix_3, out_0, vectors, near, core, far, far_z, far_core, up_bias,
    normed, activated, slope, up, attended_own, mix, out, attended,
):
    own = idx[0]
    rows, columns, block = mix_0.shape[1], near.shape[1], attended_own.shape[0]
    up[rows_at(own, rows)] = near[...]
    up[rows_at(own ^ 1, rows)] = core[0, :, :columns]
    place_halves(idx[2], up, own ^ 2, far[0, :, :columns], far_z[0, :, :columns])
    place_halves(idx[2], up, own ^ 3, far_core[0, 0, :, :columns], far_core[1, 0, :, :columns])
    for place, ref in enumerate((mix_0, mix_2, mix_1, mix_3)):
        mix[:, place * rows : (place + 1) * rows] = ref[...]
    out[:rows] = out_0[...]
    place_halves(idx[2], out, 1, far[2], far_z[2])
    out[2 * rows : 3 * rows] = core[1]
    place_halves(idx[2], out, 3, far_core[0, 1], far_core[1, 1])
    gain, shift, out_shift = vectors[2:3], vectors[3:4], vectors[4:5]
    stream = tokens[...].astype(F32) + dot(mix[...], out[...]) + out_shift
    attended[...] = stream
    normed[...] = (norm_parts(stream)[0] * gain + shift).astype(BF)
    hidden = dot(normed[...], up[...]) + up_bias[...].astype(F32)
    square = hidden * hidden
    tanh = jnp.tanh(TANH_SCALE * hidden * (1.0 + CUBIC * square))
    activated[...] = (0.5 * hidden * (1.0 + tanh)).astype(BF)
    slope[...] = 0.5 * (1.0 + tanh) + 0.5 * hidden * (1.0 - tanh * tanh) * (
        TANH_SCALE * (1.0 + 3.0 * CUBIC * square)
    )
    attended_own[...] = attended[rows_at(own, block)]


def unit_back_kernel(idx, cot_0, cot_2, cot_13, slope, down, hidden_grad, cot, bias_grad):
    own = idx[0]
    block = cot_0.shape[0]
    for bit, part in ((0, cot_0[...]), (2, cot_2[...]), (1, cot_13[:block]), (3, cot_13[block:])):
        cot[rows_at(own ^ bit, block)] = part
    grad = (dot_t(cot[...], down[...]) * slope[...]).astype(BF)
    hidden_grad[...] = grad
    bias_grad[...] = jnp.sum(grad.astype(F32), axis=0, keepdims=True)


def parts_of_rows(idx, part, keep, send):
    own = idx[0]
    block = keep.shape[0] // 2
    for place, bit in ((0, 0), (1, 2)):
        keep[place * block : (place + 1) * block] = part[rows_at(own ^ bit, block)]
    for place, bit in ((0, 1), (1, 3)):
        send[place * block : (place + 1) * block] = part[rows_at(own ^ bit, block)].astype(BF)


def norm_grad_kernel(idx, grad, weight, keep, send, part):
    part[...] = dot_t(grad[...], weight[...])
    parts_of_rows(idx, part, keep, send)


def norm_grad_sums_kernel(idx, grad, weight, tokens, keep, send, sums, part):
    result = dot_t(grad[...], weight[...])
    part[...] = result
    parts_of_rows(idx, part, keep, send)
    normal = norm_parts(tokens[...].astype(F32))[0]
    sums[0:1] = jnp.sum(result * normal, axis=0, keepdims=True)
    sums[1:2] = jnp.sum(result, axis=0, keepdims=True)


def total_kernel(idx, left, right, out):
    out[...] = left[...] + right[...]


def branch_kernel(idx, activated, down, keep, send, part):
    part[...] = dot(activated[...], down[...])
    parts_of_rows(idx, part, keep, send)


def split_rows(idx, source, groups, keep, send):
    low = idx[1]
    size = keep.shape[1] // groups
    for out, outer in ((keep, low), (send, 1 - low)):
        for half in range(2):
            for g in range(groups):
                piece = source[rows_at(4 * g + 2 * outer + half, size)]
                out[half, g * size : (g + 1) * size] = piece.astype(BF)


def unit_grads_kernel(
    idx, activated, cot, normed, hidden_grad, down_keep, down_send, up_keep, up_send, cot_sum, down_grad, up_grad
):
    units = activated.shape[1]
    down_grad[units // 8 * 8 :] = jnp.zeros((down_grad.shape[0] - units // 8 * 8, down_grad.shape[1]), F32)
    down_grad[:units] = t_dot(activated[...], cot[...])
    split_rows(idx, down_grad, 1, down_keep, down_send)
    up_grad[...] = t_dot(normed[...], hidden_grad[...])
    split_rows(idx, up_grad, 4, up_keep, up_send)
    cot_sum[...] = jnp.sum(cot[...].astype(F32), axis=0, keepdims=True)


def add_kernel(idx, keep, got, near, send):
    block = near.shape[0]
    near[...] = keep[:block] + got[:block].astype(F32)
    send[...] = (keep[block:] + got[block:].astype(F32)).astype(BF)


def output_kernel(idx, near, got, attended, vectors, out):
    out[...] = (attended[...] + near[...] + got[...].astype(F32) + vectors[5:6]).astype(BF)


def norm_back_kernel(row, idx, near, got, source, add, vectors, *outs):
    *grad, low_grad, sums = outs
    grad_in = near[...] + got[...].astype(F32)
    normal, scale = norm_parts(source[...].astype(F32))
    back, gain_sum, shift_sum = norm_back(grad_in, normal, scale, vectors[row : row + 1])
    result = add[...].astype(F32) + back
    for out in grad:
        out[...] = result
    low_grad[...] = result.astype(BF)
    sums[...] = jnp.concatenate([gain_sum, shift_sum], axis=0)


def attend_back_kernel(
    idx, grad_0, grad_2, grad_1, grad_3, out_weight, pic_col, pic_row, queries, keys, values, logs,
    branch_grad, projected_grad, sum_q, sum_v, branch_sum, mixed_grad,
):
    own = idx[0]
    block, rows = grad_0.shape[0], queries.shape[1]
    for bit, ref in zip(ORDER, (grad_0, grad_2, grad_1, grad_3)):
        branch_grad[rows_at(own ^ bit, block)] = ref[...]
    branch_sum[...] = jnp.sum(branch_grad[...].astype(F32), axis=0, keepdims=True)
    mixed_grad[...] = dot_t(branch_grad[...], out_weight[...]).astype(BF)
    allowed = allowed_of(pic_col[...], pic_row[...])
    query_parts, key_parts, value_parts = [], [], []
    for h in range(rows // HEAD_DIM):
        cut = slice(h * HEAD_DIM, (h + 1) * HEAD_DIM)
        query, key, value, grad = queries[:, cut], keys[:, cut], values[:, cut], mixed_grad[:, cut]
        scores = jnp.where(allowed, dot_t(query, key), MASKED)
        probs = jnp.exp(scores - logs[:, h : h + 1])
        probs_grad = dot_t(grad, value)
        delta = jnp.sum(probs * probs_grad, axis=-1, keepdims=True)
        scores_grad = (probs * (probs_grad - delta)).astype(BF)
        query_parts.append(dot(scores_grad, key))
        key_parts.append(t_dot(scores_grad, query))
        value_parts.append(t_dot(probs.astype(BF), grad))
    query_grad = SCALING * jnp.concatenate(query_parts, axis=1)
    value_grad = jnp.concatenate(value_parts, axis=1)
    projected_grad[:, :rows] = query_grad.astype(BF)
    projected_grad[:, rows : 2 * rows] = jnp.concatenate(key_parts, axis=1).astype(BF)
    projected_grad[:, 2 * rows :] = value_grad.astype(BF)
    sum_q[...] = jnp.sum(query_grad, axis=0, keepdims=True)
    sum_v[...] = jnp.sum(value_grad, axis=0, keepdims=True)


def fold(piece, columns):
    size = piece.shape[0] // 3
    rest = [piece[i * size : (i + 1) * size, columns:] for i in range(3)]
    return piece[:, :columns], jnp.concatenate(rest, axis=1)


def qkv_grads_kernel(
    idx, normed, projected_grad, mixed, branch_grad, sum_q, sum_v, branch_sum, cot_sum, bias_grad, sums_one, sums_two,
    keep, send, grad, out_grad, lines,
):
    rows, columns, units = sum_q.shape[1], grad.shape[1], bias_grad.shape[1]
    grad[...] = t_dot(normed[...], projected_grad[...])
    out_grad[...] = t_dot(mixed[...], branch_grad[...])

    def quarter(row):
        parts = [row[:, f * rows : (f + 1) * rows] for f in range(grad.shape[0] // rows)]
        return sum(jnp.where(idx[0] == f, part, 0.0) for f, part in enumerate(parts))

    lines[...] = jnp.zeros_like(lines)
    vectors = [sum_q[...], sum_v[...], quarter(branch_sum[...]), quarter(cot_sum[...])]
    for i, vector in enumerate(vectors):
        lines[i // 3 : i // 3 + 1, i % 3 * rows : (i % 3 + 1) * rows] = vector
    lines[2:3] = bias_grad[:, :columns]
    lines[3:4, : units - columns] = bias_grad[:, columns:]
    for i, ref in enumerate((sums_one, sums_two)):
        for j in range(2):
            at = 4 + 4 * i + 2 * j
            lines[at : at + 1] = ref[j : j + 1, :columns]
            lines[at + 1 : at + 2, :rows] = ref[j : j + 1, columns:]
    size = rows // 4
    place = grad.shape[0] // 4
    for out, outer in ((keep, idx[1]), (send, 1 - idx[1])):
        for half in range(2):
            for g in range(grad.shape[0] // rows):
                piece = grad[rows_at(4 * g + 2 * outer + half, size)]
                out[half, g * size : (g + 1) * size] = piece.astype(BF)
            upper, lower = fold(out_grad[rows_at(2 * outer + half, size)], columns)
            out[half, place : place + size] = upper.astype(BF)
            out[half, place + size : place + size + size // 3] = lower.astype(BF)
            out[half, place + size + size // 3 :] = lines[...].astype(BF)


def add_low(left, right):
    return left.astype(F32) + right.astype(F32)


def halve_kernel(idx, keep, got, keep_next, send):
    low = idx[2]
    keep_next[...] = add_low(keep[low], got[low]).astype(BF)
    send[...] = add_low(keep[1 - low], got[1 - low]).astype(BF)


def sum_kernel(idx, keep, got, out):
    out[...] = add_low(keep[...], got[...]).astype(BF)


def deal_kernel(groups, idx, keep, got, *outs):
    size = outs[0].shape[0]
    for bit in range(groups):
        cut = rows_at(idx[0] ^ bit, size)
        outs[bit][...] = add_low(keep[cut], got[cut]).astype(BF)
    place = groups * size
    for ref in outs[groups:]:
        cut = slice(place, place + ref.shape[0])
        ref[...] = add_low(keep[cut], got[cut]).astype(ref.dtype)
        place += ref.shape[0]


def join_kernel(groups, idx, *refs):
    out = refs[-1]
    size = refs[0].shape[0]
    for bit in range(groups):
        out[rows_at(idx[0] ^ bit, size)] = refs[bit][...]
    for ref in refs[groups:-1]:
        out[groups * size :] = ref[...]


def stack_kernel(idx, mine, got, out):
    out[0] = mine[...]
    out[1] = got[...]


def quarters_of(idx, mine, got):
    for outer, ref in ((idx[1], mine), (1 - idx[1], got)):
        for rel in range(2):
            inner = idx[2] if rel == 0 else 1 - idx[2]
            yield 2 * outer + inner, ref.at[rel]


def place_down_kernel(idx, mine, got, out):
    size, total = mine.shape[1], out.shape[0]
    for quarter, piece in quarters_of(idx, mine, got):

        @pl.when(quarter < 3)
        def _(quarter=quarter, piece=piece):
            out[rows_at(quarter, size)] = piece[...].astype(F32)

        @pl.when(quarter == 3)
        def _(piece=piece):
            out[3 * size :] = piece[...].astype(F32)[: total - 3 * size]


def place_up_kernel(idx, mine, got, out):
    size, columns = out.shape[0] // 4, mine.shape[2]
    for quarter, piece in quarters_of(idx, mine, got):
        for f in range(out.shape[1] // columns):
            block = piece[f * size : (f + 1) * size].astype(F32)
            out[rows_at(quarter, size), f * columns : (f + 1) * columns] = block


def place_qkv_kernel(spans, idx, mine, got, out, out_out):
    size = out.shape[0] // 4
    columns = mine.shape[2]
    place = len(spans) * size
    width = out_out.shape[1] - columns
    for quarter, piece in quarters_of(idx, mine, got):
        at = rows_at(quarter, size)
        for f, parts in enumerate(spans):
            block = piece[f * size : (f + 1) * size].astype(F32)
            for start, stop, target in parts:
                out[at, target : target + stop - start] = block[:, start:stop]
        out_out[at, :columns] = piece[place : place + size].astype(F32)
        rest = piece[place + size :].astype(F32)
        rest = jnp.concatenate([rest[:, i * width : (i + 1) * width] for i in range(3)], axis=0)
        out_out[at, columns:] = rest


def per_device(
    sizes,
    patches,
    picture,
    gain_one,
    shift_one,
    qkv_weight,
    query_bias,
    value_bias,
    out_weight,
    out_bias,
    gain_two,
    shift_two,
    up_weight,
    up_bias,
    down_weight,
    down_bias,
    cotangent,
):
    reps, shards, parts = sizes
    own = lax.axis_index("fsdp")
    low_rep, low_ctx = lax.rem(lax.axis_index("rep"), 2), lax.rem(lax.axis_index("ctx"), 2)
    idx = jnp.stack([own, low_rep, low_ctx, lax.axis_index("ctx")]).astype(jnp.int32)
    seg, width = patches.shape[1], patches.shape[2]
    total = picture.shape[1]
    rows = width // shards
    units = up_bias.shape[0]

    def swap(value, axis, bit):
        size = {"rep": reps, "fsdp": shards, "ctx": parts}[axis]
        return lax.ppermute(value, axis, [(i, i ^ bit) for i in range(size)])

    def turn(value):
        pairs = [(f * parts + c, c * parts + f) for f in range(shards) for c in range(parts)]
        return lax.ppermute(value, ("fsdp", "ctx"), pairs)

    def gather(value):
        far = swap(value, "fsdp", 2)
        return value, far, swap(value, "fsdp", 1), swap(far, "fsdp", 1)

    def scatter(keep, send, name, after=()):
        near, onward = call(
            add_kernel,
            [full_like(seg, width), low_like(seg, width)],
            (idx, keep, swap(send, "fsdp", 1)),
            name=name,
            after=after,
        )
        return near, swap(onward, "fsdp", 2)

    piece = seg // shards

    def share(*values, after):
        (value,) = call(
            join_tokens_kernel,
            [low_like(shards, len(values), piece, width)],
            (idx, *(value.reshape(shards, piece, width) for value in values)),
            name="join_tokens",
            after=after,
        )
        value = lax.all_to_all(lax.all_to_all(value, "fsdp", 0, 0), "ctx", 0, 0)
        parted = call(part_tokens_kernel, [low_like(parts, piece, width)] * len(values), (idx, value), name="part_tokens")
        return [value.reshape(seg, width) for value in parted]

    def share_back(*values):
        value = jnp.stack([value.reshape(parts, piece, width) for value in values], axis=1)
        value = lax.all_to_all(lax.all_to_all(value, "ctx", 0, 0), "fsdp", 0, 0)
        return [value[:, i].reshape(seg, width) for i in range(len(values))]

    def spread(near, core, far_two, far_three):
        far_two, far_three = swap(far_two, "fsdp", 2), swap(far_three, "fsdp", 3)
        return near, swap(core, "fsdp", 1), far_two, swap(far_two, "rep", 1), far_three, swap(far_three, "rep", 1)

    pic = turn(picture[0]).reshape(parts, shards, piece).transpose(1, 0, 2).reshape(total)
    pic_col, pic_row = pic[:, None], pic[None, :]
    vectors_own = jnp.stack([gain_one, shift_one, gain_two, shift_two, out_bias, down_bias])
    vectors_own = jnp.pad(vectors_own, ((0, EXTRA - vectors_own.shape[0]), (0, 0)))
    qkv_spans = tuple(
        tuple((s * width + f * rows, s * width + (f + 1) * rows) for s in range(3)) for f in range(shards)
    )
    up_spans = tuple(((f * units, (f + 1) * units),) for f in range(shards))
    up_near, core, far = call(
        functools.partial(cut_both_kernel, up_spans),
        [low_like(rows, units), low_like(2, rows, width), low_like(3, rows // 2, width)],
        (idx, up_weight, out_weight),
        [pltpu.VMEM((shards, rows, units), BF)],
        name="cut_up",
    )
    core, far = swap(core, "fsdp", 1), swap(far, "fsdp", 2)
    far_z = swap(far, "ctx", 1)
    far_core = swap(jnp.stack([far[1:], far_z[1:]]), "fsdp", 1)
    tokens_own, cot_own = share(patches[0], cotangent[0], after=(up_near,))
    qkv_parts = spread(
        *call(
            functools.partial(cut_kernel, qkv_spans),
            [low_like(rows + EXTRA, 3 * rows)] * 2 + [low_like(rows // 2 + EXTRA, 3 * rows)] * 2,
            (idx, qkv_weight, vectors_own),
            [pltpu.VMEM((shards, rows, 3 * rows), BF)],
            name="cut_qkv",
            after=(up_near,),
        )
    )
    token_parts = gather(tokens_own)

    cot_two = swap(cot_own, "fsdp", 2)
    cot_others = swap(jnp.concatenate([cot_own, cot_two], axis=0), "fsdp", 1)

    tokens, normed_one, qkv_own, vectors, queries, keys, values, mixed, logs = call(
        project_kernel,
        [
            low_like(total, width),
            low_like(total, width),
            low_like(width, 3 * rows),
            full_like(8, width),
            low_like(total, rows),
            low_like(total, rows),
            low_like(total, rows),
            low_like(total, rows),
            full_like(total, rows // HEAD_DIM),
        ],
        (idx, *token_parts, *qkv_parts, pic_col, pic_row, query_bias[None], value_bias[None]),
        [pltpu.VMEM((shards, 8, rows), F32)],
        name="project",
        us=10,
    )
    mixed_parts = gather(mixed)
    normed_two, activated, slope, up_own, attended_own = call(
        unit_kernel,
        [
            low_like(total, width),
            low_like(total, units),
            full_like(total, units),
            low_like(width, units),
            full_like(seg, width),
        ],
        (
            idx, tokens, *mixed_parts, out_weight, vectors, up_near, core, far, far_z, far_core, up_bias[None],
        ),
        [pltpu.VMEM((total, width), BF), pltpu.VMEM((width, width), BF), pltpu.VMEM((total, width), F32)],
        name="units",
        us=12,
    )
    hidden_grad, cot, up_bias_grad = call(
        unit_back_kernel,
        [low_like(total, units), low_like(total, width), full_like(1, units)],
        (idx, cot_own, cot_two, cot_others, slope, down_weight),
        name="unit_back",
        us=5,
    )

    padded = (units + 63) // 64 * 64
    sums = {}
    last_steps = [(axis, 2**i) for axis, size in (("rep", reps), ("ctx", parts)) for i in range(1, size.bit_length() - 1)]

    def step(name, number, after):
        keep, got = sums[name]
        run = functools.partial(call, after=after, name=f"{name}_{number}")
        if number == 1:
            value, send = run(halve_kernel, [low_like(*keep.shape[1:])] * 2, (idx, keep, got))
            sums[name] = value, swap(send, "ctx", 1)
        elif number == 2:
            (value,) = run(sum_kernel, [low_like(*keep.shape)], (idx, keep, got))
            for axis, bit in last_steps[:-1]:
                (value,) = call(sum_kernel, [low_like(*keep.shape)], (idx, value, swap(value, axis, bit)), name="more")
            sums[name] = value, swap(value, *last_steps[-1])
        elif number == 3 and name == "d":
            (value,) = run(sum_kernel, [low_like(*keep.shape)], (idx, keep, got))
            sums[name] = value, swap(value, "ctx", 1)
        elif number == 3:
            outs = [low_like(rows // 4, keep.shape[1])] * shards
            if name == "q":
                outs += [low_like(rows // 3, keep.shape[1]), full_like(EXTRA, keep.shape[1])]
            outs = run(functools.partial(deal_kernel, shards), outs, (idx, keep, got))
            value = outs[0]
            dealt = [value] + [swap(outs[bit], "fsdp", bit) for bit in range(1, shards)]
            sums[name] = dealt + list(outs[shards : shards + 1]), None
            if name == "q":
                val["lines"] = outs[shards + 1]
        elif number == 4 and name != "d":
            total_rows = sum(part.shape[0] for part in keep)
            (value,) = run(
                functools.partial(join_kernel, shards), [low_like(total_rows, keep[0].shape[1])], (idx, *keep)
            )
            sums[name] = value, swap(value, "ctx", 1)
        else:
            (value,) = run(stack_kernel, [low_like(2, *keep.shape)], (idx, keep, got))
            sums[name] = value, swap(value, "rep", 1)
        return value

    qkv_places = tuple(
        tuple((s * rows, (s + 1) * rows, s * width + f * rows) for s in range(3)) for f in range(shards)
    )
    val = {}
    cut = lambda full: lax.dynamic_slice_in_dim(full, own * rows, rows, 1)
    shared = [full_like(2 * seg, width), low_like(2 * seg, width)]

    def run_unit_grads(after):
        down_keep, down_send, up_keep, up_send, val["cot_sum"] = call(
            unit_grads_kernel,
            [low_like(2, padded // 4, width)] * 2 + [low_like(2, rows, units)] * 2 + [full_like(1, width)],
            (idx, activated, cot, normed_two, hidden_grad),
            [pltpu.VMEM((padded, width), F32), pltpu.VMEM((width, units), F32)],
            name="unit_grads",
        us=8,
            after=after,
        )
        sums["d"] = down_keep, swap(down_send, "rep", 1)
        sums["u"] = up_keep, swap(up_send, "rep", 1)
        return val["cot_sum"]

    def run_norm_two_grad(after):
        keep, send = call(
            norm_grad_kernel,
            shared,
            (idx, hidden_grad, up_own),
            [pltpu.VMEM((total, width), F32)],
            name="norm_two_grad",
        us=4,
            after=after,
        )
        val["two"] = keep, swap(send, "fsdp", 1)
        return keep

    def run_branch(after):
        keep, send = call(
            branch_kernel,
            shared,
            (idx, activated, down_weight),
            [pltpu.VMEM((total, width), F32)],
            name="branch",
        us=4,
            after=after,
        )
        val["out"] = keep, swap(send, "fsdp", 1)
        return keep

    def run_add(key, after):
        near, onward = call(
            add_kernel,
            [full_like(seg, width), low_like(seg, width)],
            (idx, *val[key]),
            name="add_" + key,
            after=after,
        )
        val[key] = near, swap(onward, "fsdp", 2)
        return near

    def run_norm_two_back(after):
        val["attended_grad"], low_grad, val["sums_two"] = call(
            functools.partial(norm_back_kernel, 2),
            [full_like(seg, width), low_like(seg, width), full_like(2, width)],
            (idx, *val["two"], attended_own, cot_own, vectors),
            name="norm_two_back",
            after=after,
        )
        val["branch_grad"] = gather(low_grad)
        return val["sums_two"]

    def run_attend_back(after):
        val["branch_grad"], val["projected_grad"], val["sum_q"], val["sum_v"], val["branch_sum"] = call(
            attend_back_kernel,
            [
                low_like(total, width),
                low_like(total, 3 * rows),
                full_like(1, rows),
                full_like(1, rows),
                full_like(1, width),
            ],
            (idx, *val["branch_grad"], out_weight, pic_col, pic_row, queries, keys, values, logs),
            [pltpu.VMEM((total, rows), BF)],
            name="attend_back",
        us=9,
            after=after,
        )
        return val["sum_q"]

    def run_qkv_grads(after):
        names = ("sum_q", "sum_v", "branch_sum", "cot_sum")
        keep, send = call(
            qkv_grads_kernel,
            [low_like(2, rows + rows // 3 + EXTRA, 3 * rows)] * 2,
            (
                idx, normed_one, val["projected_grad"], mixed, val["branch_grad"], *(val[name] for name in names),
                up_bias_grad, val["sums_one"], val["sums_two"],
            ),
            [pltpu.VMEM((width, 3 * rows), F32), pltpu.VMEM((rows, width), F32), pltpu.VMEM((EXTRA, 3 * rows), F32)],
            name="qkv_grads",
        us=5,
            after=after,
        )
        sums["q"] = keep, swap(send, "rep", 1)
        return keep

    def run_norm_one_grad(after):
        keep, send, val["sums_one"] = call(
            norm_grad_sums_kernel,
            shared + [full_like(2, width)],
            (idx, val["projected_grad"], qkv_own, tokens),
            [pltpu.VMEM((total, width), F32)],
            name="norm_one_grad",
        us=4,
            after=after,
        )
        val["one"] = keep, swap(send, "fsdp", 1)
        return keep

    def run_norm_one_back(after):
        low_grad, _ = call(
            functools.partial(norm_back_kernel, 0),
            [low_like(seg, width), full_like(2, width)],
            (idx, *val["one"], tokens_own, val["attended_grad"], vectors),
            name="norm_one_back",
            after=after,
        )
        val["input_grad"] = low_grad
        return low_grad

    def run_output(after):
        (low,) = call(
            output_kernel, [low_like(seg, width)], (idx, *val["out"], attended_own, vectors), name="output", after=after
        )
        val["output"] = low
        return low

    def run_lines(number, after):
        if number > 1:
            (val["lines"],) = call(
                total_kernel,
                [full_like(*val["lines"].shape)],
                (idx, *val["lines_parts"]),
                name=f"lines_{number}",
                after=after,
            )
        else:
            val["own_lines"] = val["lines"]
        if number < 3:
            val["lines_parts"] = val["lines"], swap(val["lines"], "fsdp", number)
        return val["lines"]

    def run_share_back(after):
        val["output"], val["input_grad"] = share_back(val["output"], val["input_grad"])
        return after[0]

    def run_place(key, after):
        run = functools.partial(call, name="place_" + key, after=after)
        if key == "d":
            (val["d"],) = run(place_down_kernel, [full_like(units, width)], (idx, *sums["d"]))
        elif key == "u":
            (val["u"],) = run(place_up_kernel, [full_like(rows, shards * units)], (idx, *sums["u"]))
        else:
            outs = [full_like(rows, 3 * width), full_like(rows, width)]
            val["q"], val["o"] = run(functools.partial(place_qkv_kernel, qkv_places), outs, (idx, *sums["q"]))
        return val[key]

    tasks = {
        "ugrads": run_unit_grads,
        "ng2": run_norm_two_grad,
        "br": run_branch,
        "add2": functools.partial(run_add, "two"),
        "addo": functools.partial(run_add, "out"),
        "add1": functools.partial(run_add, "one"),
        "K3": run_norm_two_back,
        "K4": run_attend_back,
        "K5": run_norm_one_back,
        "fin": run_output,
        "back": run_share_back,
        "qg": run_qkv_grads,
        "ng1": run_norm_one_grad,
    }
    token = (hidden_grad,)
    for name in SCHEDULE:
        if name in tasks:
            token = (tasks[name](token),)
        elif name.startswith("place_"):
            token = (run_place(name[6:], token),)
        elif name.startswith("v"):
            token = (run_lines(int(name[1:]), token),)
        else:
            token = (step(name[:-1], int(name[-1]), token),)
    lines, own_lines = val["lines"], val["own_lines"]
    vector_of = lambda i: own_lines[i // 3, i % 3 * rows : (i % 3 + 1) * rows]
    norms = jnp.concatenate([lines[4:12:2], lines[5:12:2, :rows]], axis=1)
    norms = lax.dynamic_slice_in_dim(norms, own * rows, rows, 1)
    return (
        val["output"][None],
        val["input_grad"][None],
        norms[0],
        norms[1],
        val["q"],
        vector_of(0),
        vector_of(1),
        val["o"],
        vector_of(2),
        norms[2],
        norms[3],
        val["u"],
        own_lines[2:4].reshape(-1)[:units],
        val["d"],
        vector_of(3),
    )


def solution(mesh):
    sizes = tuple(mesh.shape[axis] for axis in ("rep", "fsdp", "ctx"))
    tokens = P(("rep", "fsdp"), "ctx", None)
    vector, matrix = P("fsdp"), P("fsdp", None)
    return jax.shard_map(
        functools.partial(per_device, sizes),
        mesh=mesh,
        in_specs=(
            tokens,
            P(("rep", "fsdp"), None),
            vector,
            vector,
            matrix,
            vector,
            vector,
            matrix,
            vector,
            vector,
            vector,
            matrix,
            vector,
            matrix,
            vector,
            tokens,
        ),
        out_specs=(
            tokens,
            tokens,
            vector,
            vector,
            matrix,
            vector,
            vector,
            matrix,
            vector,
            vector,
            vector,
            matrix,
            vector,
            matrix,
            vector,
        ),
        check_vma=False,
    )
```

```python
import functools

import jax
import jax.numpy as jnp
from jax import lax
from jax.experimental import pallas as pl
from jax.experimental.pallas import tpu as pltpu
from jax.sharding import PartitionSpec as P

HEADS = 16
HEAD_DIM = 72
PICS = 3

EPSILON = 1e-06
MASKED = -1e30
BF = jnp.bfloat16
F32 = jnp.float32
SCALING = HEAD_DIM ** (-0.5)
TANH_SCALE = (2.0 / jnp.pi) ** 0.5
CUBIC = 0.044715
VMEM_LIMIT = 32 * 2**20
ORDER = (0, 2, 1, 3)
SCHEDULE = (
    "ng2", "ugrads", "add2", "br", "K3", "d1", "K4", "addo", "ng1", "d2", "qg", "u1", "add1", "d3", "fin",
    "u2", "K5", "d4", "q1", "u3", "q2", "u4", "back", "u5", "place_d", "q3", "q4", "v1", "place_u", "v2",
    "v3", "outs", "place_q",
)
EXTRA = 16


def dot(left, right):
    return jnp.dot(left, right, preferred_element_type=F32)


def dot_t(left, right):
    return lax.dot_general(left, right, (((1,), (1,)), ((), ())), preferred_element_type=F32)


def t_dot(left, right):
    return lax.dot_general(left, right, (((0,), (0,)), ((), ())), preferred_element_type=F32)


def rows_at(index, size):
    return pl.ds(pl.multiple_of(index * size, 8), size)


def norm_parts(values):
    center = values - jnp.mean(values, axis=-1, keepdims=True)
    spread = jnp.mean(center * center, axis=-1, keepdims=True)
    scale = lax.rsqrt(spread + EPSILON)
    return center * scale, scale


def norm_back(grad, normal, scale, gain):
    through = grad * gain
    mean_one = jnp.mean(through, axis=-1, keepdims=True)
    mean_two = jnp.mean(through * normal, axis=-1, keepdims=True)
    back = scale * (through - mean_one - normal * mean_two)
    return back, jnp.sum(grad * normal, axis=0, keepdims=True), jnp.sum(grad, axis=0, keepdims=True)


def call(kernel, outs, ins, scratch=(), name=None, after=(), us=1):
    vmem = pl.BlockSpec(memory_space=pltpu.VMEM)
    skip = len(after)

    def body(*refs):
        kernel(*refs[skip:])

    return pl.pallas_call(
        body,
        out_shape=outs,
        in_specs=[pl.BlockSpec(memory_space=pl.ANY)] * skip
        + [pl.BlockSpec(memory_space=pltpu.SMEM)]
        + [vmem] * (len(ins) - 1),
        out_specs=[vmem] * len(outs),
        scratch_shapes=list(scratch),
        compiler_params=pltpu.CompilerParams(vmem_limit_bytes=VMEM_LIMIT),
        cost_estimate=pl.CostEstimate(flops=us * 10**9, bytes_accessed=0, transcendentals=0),
        name=name,
    )(*after, *ins)


def low_like(*shape):
    return jax.ShapeDtypeStruct(shape, BF)


def full_like(*shape):
    return jax.ShapeDtypeStruct(shape, F32)


def cut_columns(spans, weight, stack):
    for f, parts in enumerate(spans):
        place = 0
        for start, stop in parts:
            stack[f, :, place : place + stop - start] = weight[:, start:stop]
            place += stop - start


def cut_kernel(spans, idx, weight, vectors, near, core, far_two, far_three, stack):
    rows = weight.shape[0]
    own, low = idx[0], idx[1]
    cut_columns(spans, weight, stack)
    for bit, out in enumerate((near, core, far_two, far_three)):
        size = out.shape[0] - EXTRA
        out[:size] = stack[own ^ bit] if size == rows else stack[own ^ bit, rows_at(low, size)]
        out[size:] = jnp.zeros((EXTRA, out.shape[1]), BF)
        out[size:, : vectors.shape[1]] = vectors[...]


def cut_both_kernel(spans, idx, weight, out_weight, near, core, far, stack):
    own, low = idx[0], idx[2]
    half = weight.shape[0] // 2
    columns = weight.shape[1] // len(spans)
    cut_columns(spans, weight, stack)
    near[...] = stack[own]
    core[0, :, :columns] = stack[own ^ 1]
    core[1] = out_weight[...]
    far[0, :, :columns] = stack[own ^ 2, rows_at(low, half)]
    far[1, :, :columns] = stack[own ^ 3, rows_at(low, half)]
    far[2] = out_weight[rows_at(low, half)]


def place_halves(low, target, block, mine, other):
    half = mine.shape[0]
    target[rows_at(2 * block + low, half)] = mine
    target[rows_at(2 * block + 1 - low, half)] = other


def join_tokens_kernel(idx, *refs):
    for i, ref in enumerate(refs[:-1]):
        for f in range(ref.shape[0]):
            refs[-1][f, i] = ref[f]


def part_tokens_kernel(idx, source, *outs):
    for i, out in enumerate(outs):
        for c in range(out.shape[0]):
            out[c] = source[c, i]


def allowed_of(pic_col, pic_row):
    total = pic_row.shape[1]
    rows = lax.broadcasted_iota(jnp.int32, (total, total), 0)
    columns = lax.broadcasted_iota(jnp.int32, (total, total), 1)
    return (pic_col == pic_row) & ((pic_row != PICS) | (rows == columns))


def project_kernel(
    idx, tok_0, tok_2, tok_1, tok_3, near, core, far_two, far_two_y, far_three, far_three_y, pic_col, pic_row, query_bias, value_bias,
    tokens, normed, weight, vectors, queries, keys, values, mixed, logs, pieces,
):
    own = idx[0]
    rows = queries.shape[1]
    block = tok_0.shape[0]
    half = rows // 2
    weight[rows_at(own, rows)] = near[:rows]
    weight[rows_at(own ^ 1, rows)] = core[:rows]
    place_halves(idx[1], weight, own ^ 2, far_two[:half], far_two_y[:half])
    place_halves(idx[1], weight, own ^ 3, far_three[:half], far_three_y[:half])
    for bit, ref in enumerate((near, core, far_two, far_three)):
        pieces[bit] = ref[ref.shape[0] - EXTRA :, :rows].astype(F32)[:8]
    vectors[...] = jnp.concatenate([pieces[own ^ f] for f in range(len(ORDER))], axis=1)
    gain, shift = vectors[0:1], vectors[1:2]
    for bit, ref in zip(ORDER, (tok_0, tok_2, tok_1, tok_3)):
        part = ref[...]
        tokens[rows_at(own ^ bit, block)] = part
        normed[rows_at(own ^ bit, block)] = (norm_parts(part.astype(F32))[0] * gain + shift).astype(BF)
    query_add, value_add = query_bias[...].astype(F32), value_bias[...].astype(F32)

    result = dot(normed[...], weight[...])
    queries[...] = (SCALING * (result[:, :rows] + query_add)).astype(BF)
    keys[...] = result[:, rows : 2 * rows].astype(BF)
    values[...] = (result[:, 2 * rows :] + value_add).astype(BF)
    allowed = allowed_of(pic_col[...], pic_row[...])
    outs, log_parts = [], []
    for h in range(rows // HEAD_DIM):
        cut = slice(h * HEAD_DIM, (h + 1) * HEAD_DIM)
        scores = jnp.where(allowed, dot_t(queries[:, cut], keys[:, cut]), MASKED)
        largest = jnp.max(scores, axis=-1, keepdims=True)
        expo = jnp.exp(scores - largest)
        sums = jnp.sum(expo, axis=-1, keepdims=True)
        probs = (expo * (1.0 / sums)).astype(BF)
        outs.append(dot(probs, values[:, cut]))
        log_parts.append(largest + jnp.log(sums))
    mixed[...] = jnp.concatenate(outs, axis=1).astype(BF)
    logs[...] = jnp.concatenate(log_parts, axis=1)


def unit_kernel(
    idx, tokens, mix_0, mix_2, mix_1, mix_3, out_0, vectors, near, core, far, far_z, far_core, up_bias,
    normed, activated, slope, up, attended_own, mix, out, attended,
):
    own = idx[0]
    rows, columns, block = mix_0.shape[1], near.shape[1], attended_own.shape[0]
    up[rows_at(own, rows)] = near[...]
    up[rows_at(own ^ 1, rows)] = core[0, :, :columns]
    place_halves(idx[2], up, own ^ 2, far[0, :, :columns], far_z[0, :, :columns])
    place_halves(idx[2], up, own ^ 3, far_core[0, 0, :, :columns], far_core[1, 0, :, :columns])
    for place, ref in enumerate((mix_0, mix_2, mix_1, mix_3)):
        mix[:, place * rows : (place + 1) * rows] = ref[...]
    out[:rows] = out_0[...]
    place_halves(idx[2], out, 1, far[2], far_z[2])
    out[2 * rows : 3 * rows] = core[1]
    place_halves(idx[2], out, 3, far_core[0, 1], far_core[1, 1])
    gain, shift, out_shift = vectors[2:3], vectors[3:4], vectors[4:5]
    stream = tokens[...].astype(F32) + dot(mix[...], out[...]) + out_shift
    attended[...] = stream
    normed[...] = (norm_parts(stream)[0] * gain + shift).astype(BF)
    hidden = dot(normed[...], up[...]) + up_bias[...].astype(F32)
    square = hidden * hidden
    tanh = jnp.tanh(TANH_SCALE * hidden * (1.0 + CUBIC * square))
    activated[...] = (0.5 * hidden * (1.0 + tanh)).astype(BF)
    slope[...] = 0.5 * (1.0 + tanh) + 0.5 * hidden * (1.0 - tanh * tanh) * (
        TANH_SCALE * (1.0 + 3.0 * CUBIC * square)
    )
    attended_own[...] = attended[rows_at(own, block)]


def unit_back_kernel(idx, cot_0, cot_2, cot_13, slope, down, hidden_grad, cot, bias_grad):
    own = idx[0]
    block = cot_0.shape[0]
    for bit, part in ((0, cot_0[...]), (2, cot_2[...]), (1, cot_13[:block]), (3, cot_13[block:])):
        cot[rows_at(own ^ bit, block)] = part
    grad = (dot_t(cot[...], down[...]) * slope[...]).astype(BF)
    hidden_grad[...] = grad
    bias_grad[...] = jnp.sum(grad.astype(F32), axis=0, keepdims=True)


def parts_of_rows(idx, part, keep, send):
    own = idx[0]
    block = keep.shape[0] // 2
    for place, bit in ((0, 0), (1, 2)):
        keep[place * block : (place + 1) * block] = part[rows_at(own ^ bit, block)]
    for place, bit in ((0, 1), (1, 3)):
        send[place * block : (place + 1) * block] = part[rows_at(own ^ bit, block)].astype(BF)


def norm_grad_kernel(idx, grad, weight, keep, send, part):
    part[...] = dot_t(grad[...], weight[...])
    parts_of_rows(idx, part, keep, send)


def norm_grad_sums_kernel(idx, grad, weight, tokens, keep, send, sums, part):
    result = dot_t(grad[...], weight[...])
    part[...] = result
    parts_of_rows(idx, part, keep, send)
    normal = norm_parts(tokens[...].astype(F32))[0]
    sums[0:1] = jnp.sum(result * normal, axis=0, keepdims=True)
    sums[1:2] = jnp.sum(result, axis=0, keepdims=True)


def total_kernel(idx, left, right, out):
    out[...] = left[...] + right[...]


def branch_kernel(idx, activated, down, keep, send, part):
    part[...] = dot(activated[...], down[...])
    parts_of_rows(idx, part, keep, send)


def split_rows(idx, source, groups, keep, send):
    low = idx[1]
    size = keep.shape[1] // groups
    for out, outer in ((keep, low), (send, 1 - low)):
        for half in range(2):
            for g in range(groups):
                piece = source[rows_at(4 * g + 2 * outer + half, size)]
                out[half, g * size : (g + 1) * size] = piece.astype(BF)


def unit_grads_kernel(
    idx, activated, cot, normed, hidden_grad, down_keep, down_send, up_keep, up_send, cot_sum, down_grad, up_grad
):
    units = activated.shape[1]
    down_grad[units // 8 * 8 :] = jnp.zeros((down_grad.shape[0] - units // 8 * 8, down_grad.shape[1]), F32)
    down_grad[:units] = t_dot(activated[...], cot[...])
    split_rows(idx, down_grad, 1, down_keep, down_send)
    up_grad[...] = t_dot(normed[...], hidden_grad[...])
    split_rows(idx, up_grad, 4, up_keep, up_send)
    cot_sum[...] = jnp.sum(cot[...].astype(F32), axis=0, keepdims=True)


def add_kernel(idx, keep, got, near, send):
    block = near.shape[0]
    near[...] = keep[:block] + got[:block].astype(F32)
    send[...] = (keep[block:] + got[block:].astype(F32)).astype(BF)


def output_kernel(idx, near, got, attended, vectors, out):
    out[...] = (attended[...] + near[...] + got[...].astype(F32) + vectors[5:6]).astype(BF)


def norm_back_kernel(row, idx, near, got, source, add, vectors, *outs):
    *grad, low_grad, sums = outs
    grad_in = near[...] + got[...].astype(F32)
    normal, scale = norm_parts(source[...].astype(F32))
    back, gain_sum, shift_sum = norm_back(grad_in, normal, scale, vectors[row : row + 1])
    result = add[...].astype(F32) + back
    for out in grad:
        out[...] = result
    low_grad[...] = result.astype(BF)
    sums[...] = jnp.concatenate([gain_sum, shift_sum], axis=0)


def attend_back_kernel(
    idx, grad_0, grad_2, grad_1, grad_3, out_weight, pic_col, pic_row, queries, keys, values, logs,
    branch_grad, projected_grad, sum_q, sum_v, branch_sum, mixed_grad,
):
    own = idx[0]
    block, rows = grad_0.shape[0], queries.shape[1]
    for bit, ref in zip(ORDER, (grad_0, grad_2, grad_1, grad_3)):
        branch_grad[rows_at(own ^ bit, block)] = ref[...]
    branch_sum[...] = jnp.sum(branch_grad[...].astype(F32), axis=0, keepdims=True)
    mixed_grad[...] = dot_t(branch_grad[...], out_weight[...]).astype(BF)
    allowed = allowed_of(pic_col[...], pic_row[...])
    query_parts, key_parts, value_parts = [], [], []
    for h in range(rows // HEAD_DIM):
        cut = slice(h * HEAD_DIM, (h + 1) * HEAD_DIM)
        query, key, value, grad = queries[:, cut], keys[:, cut], values[:, cut], mixed_grad[:, cut]
        scores = jnp.where(allowed, dot_t(query, key), MASKED)
        probs = jnp.exp(scores - logs[:, h : h + 1])
        probs_grad = dot_t(grad, value)
        delta = jnp.sum(probs * probs_grad, axis=-1, keepdims=True)
        scores_grad = (probs * (probs_grad - delta)).astype(BF)
        query_parts.append(dot(scores_grad, key))
        key_parts.append(t_dot(scores_grad, query))
        value_parts.append(t_dot(probs.astype(BF), grad))
    query_grad = SCALING * jnp.concatenate(query_parts, axis=1)
    value_grad = jnp.concatenate(value_parts, axis=1)
    projected_grad[:, :rows] = query_grad.astype(BF)
    projected_grad[:, rows : 2 * rows] = jnp.concatenate(key_parts, axis=1).astype(BF)
    projected_grad[:, 2 * rows :] = value_grad.astype(BF)
    sum_q[...] = jnp.sum(query_grad, axis=0, keepdims=True)
    sum_v[...] = jnp.sum(value_grad, axis=0, keepdims=True)


def fold(piece, columns):
    size = piece.shape[0] // 3
    rest = [piece[i * size : (i + 1) * size, columns:] for i in range(3)]
    return piece[:, :columns], jnp.concatenate(rest, axis=1)


def quarter_places(idx):
    rep, ctx = idx[1], idx[2]
    return 2 * rep + ctx, 2 * (1 - rep) + ctx, 2 * rep + 1 - ctx, 2 * (1 - rep) + 1 - ctx


def qkv_grads_kernel(
    idx, normed, projected_grad, mixed, branch_grad, sum_q, sum_v, branch_sum, cot_sum, bias_grad, sums_one, sums_two,
    keep, send, grad, out_grad, lines,
):
    rows, columns, units = sum_q.shape[1], grad.shape[1], bias_grad.shape[1]
    grad[...] = t_dot(normed[...], projected_grad[...])
    out_grad[...] = t_dot(mixed[...], branch_grad[...])

    def quarter(row):
        parts = [row[:, f * rows : (f + 1) * rows] for f in range(grad.shape[0] // rows)]
        return sum(jnp.where(idx[0] == f, part, 0.0) for f, part in enumerate(parts))

    lines[...] = jnp.zeros_like(lines)
    vectors = [sum_q[...], sum_v[...], quarter(branch_sum[...]), quarter(cot_sum[...])]
    for i, vector in enumerate(vectors):
        lines[i // 3 : i // 3 + 1, i % 3 * rows : (i % 3 + 1) * rows] = vector
    lines[2:3] = bias_grad[:, :columns]
    lines[3:4, : units - columns] = bias_grad[:, columns:]
    for i, ref in enumerate((sums_one, sums_two)):
        for j in range(2):
            at = 4 + 4 * i + 2 * j
            lines[at : at + 1] = ref[j : j + 1, :columns]
            lines[at + 1 : at + 2, :rows] = ref[j : j + 1, columns:]
    size = rows // 4
    place = grad.shape[0] // 4
    for out, outer in ((keep, idx[1]), (send, 1 - idx[1])):
        for half in range(2):
            for g in range(grad.shape[0] // rows):
                piece = grad[rows_at(4 * g + 2 * outer + half, size)]
                out[half, g * size : (g + 1) * size] = piece.astype(BF)
            upper, lower = fold(out_grad[rows_at(2 * outer + half, size)], columns)
            out[half, place : place + size] = upper.astype(BF)
            out[half, place + size : place + size + size // 3] = lower.astype(BF)
            out[half, place + size + size // 3 :] = lines[...].astype(BF)


def add_low(left, right):
    return left.astype(F32) + right.astype(F32)


def halve_kernel(idx, keep, got, keep_next, send):
    low = idx[2]
    keep_next[...] = add_low(keep[low], got[low]).astype(BF)
    send[...] = add_low(keep[1 - low], got[1 - low]).astype(BF)


def sum_kernel(idx, keep, got, out):
    out[...] = add_low(keep[...], got[...]).astype(BF)


def deal_kernel(groups, idx, keep, got, *outs):
    size = outs[0].shape[0]
    for bit in range(groups):
        cut = rows_at(idx[0] ^ bit, size)
        outs[bit][...] = add_low(keep[cut], got[cut]).astype(BF)
    place = groups * size
    for ref in outs[groups:]:
        cut = slice(place, place + ref.shape[0])
        ref[...] = add_low(keep[cut], got[cut]).astype(ref.dtype)
        place += ref.shape[0]


def join_kernel(groups, idx, *refs):
    out = refs[-1]
    size = refs[0].shape[0]
    for bit in range(groups):
        out[rows_at(idx[0] ^ bit, size)] = refs[bit][...]
    for ref in refs[groups:-1]:
        out[groups * size :] = ref[...]


def stack_kernel(idx, mine, got, out):
    out[0] = mine[...]
    out[1] = got[...]


def quarters_of(idx, mine, got):
    for outer, ref in ((idx[1], mine), (1 - idx[1], got)):
        for rel in range(2):
            inner = idx[2] if rel == 0 else 1 - idx[2]
            yield 2 * outer + inner, ref.at[rel]


def place_down_kernel(idx, mine, got, out):
    size, total = mine.shape[1], out.shape[0]
    for quarter, piece in quarters_of(idx, mine, got):

        @pl.when(quarter < 3)
        def _(quarter=quarter, piece=piece):
            out[rows_at(quarter, size)] = piece[...].astype(F32)

        @pl.when(quarter == 3)
        def _(piece=piece):
            out[3 * size :] = piece[...].astype(F32)[: total - 3 * size]


def place_up_kernel(idx, mine, got, out):
    size, columns = out.shape[0] // 4, mine.shape[2]
    for quarter, piece in quarters_of(idx, mine, got):
        for f in range(out.shape[1] // columns):
            block = piece[f * size : (f + 1) * size].astype(F32)
            out[rows_at(quarter, size), f * columns : (f + 1) * columns] = block


def place_qkv_kernel(spans, idx, own, from_rep, from_ctx, from_both, out, out_out):
    size = out.shape[0] // 4
    columns = own.shape[1]
    place = len(spans) * size
    width = out_out.shape[1] - columns
    for quarter, piece in zip(quarter_places(idx), (own, from_rep, from_ctx, from_both)):
        at = rows_at(quarter, size)
        for f, parts in enumerate(spans):
            block = piece[f * size : (f + 1) * size].astype(F32)
            for start, stop, target in parts:
                out[at, target : target + stop - start] = block[:, start:stop]
        out_out[at, :columns] = piece[place : place + size].astype(F32)
        rest = piece[place + size :].astype(F32)
        rest = jnp.concatenate([rest[:, i * width : (i + 1) * width] for i in range(3)], axis=0)
        out_out[at, columns:] = rest


def per_device(
    sizes,
    patches,
    picture,
    gain_one,
    shift_one,
    qkv_weight,
    query_bias,
    value_bias,
    out_weight,
    out_bias,
    gain_two,
    shift_two,
    up_weight,
    up_bias,
    down_weight,
    down_bias,
    cotangent,
):
    reps, shards, parts = sizes
    own = lax.axis_index("fsdp")
    low_rep, low_ctx = lax.rem(lax.axis_index("rep"), 2), lax.rem(lax.axis_index("ctx"), 2)
    idx = jnp.stack([own, low_rep, low_ctx, lax.axis_index("ctx")]).astype(jnp.int32)
    seg, width = patches.shape[1], patches.shape[2]
    total = picture.shape[1]
    rows = width // shards
    units = up_bias.shape[0]

    def swap(value, axis, bit):
        size = {"rep": reps, "fsdp": shards, "ctx": parts}[axis]
        return lax.ppermute(value, axis, [(i, i ^ bit) for i in range(size)])

    def turn(value):
        pairs = [(f * parts + c, c * parts + f) for f in range(shards) for c in range(parts)]
        return lax.ppermute(value, ("fsdp", "ctx"), pairs)

    def gather(value):
        far = swap(value, "fsdp", 2)
        return value, far, swap(value, "fsdp", 1), swap(far, "fsdp", 1)

    def scatter(keep, send, name, after=()):
        near, onward = call(
            add_kernel,
            [full_like(seg, width), low_like(seg, width)],
            (idx, keep, swap(send, "fsdp", 1)),
            name=name,
            after=after,
        )
        return near, swap(onward, "fsdp", 2)

    piece = seg // shards

    def share(*values, after):
        (value,) = call(
            join_tokens_kernel,
            [low_like(shards, len(values), piece, width)],
            (idx, *(value.reshape(shards, piece, width) for value in values)),
            name="join_tokens",
            after=after,
        )
        value = lax.all_to_all(lax.all_to_all(value, "fsdp", 0, 0), "ctx", 0, 0)
        parted = call(part_tokens_kernel, [low_like(parts, piece, width)] * len(values), (idx, value), name="part_tokens")
        return [value.reshape(seg, width) for value in parted]

    def share_back(*values):
        value = jnp.stack([value.reshape(parts, piece, width) for value in values], axis=1)
        return lax.all_to_all(lax.all_to_all(value, "ctx", 0, 0), "fsdp", 0, 0)

    def spread(near, core, far_two, far_three):
        far_two, far_three = swap(far_two, "fsdp", 2), swap(far_three, "fsdp", 3)
        return near, swap(core, "fsdp", 1), far_two, swap(far_two, "rep", 1), far_three, swap(far_three, "rep", 1)

    pic = turn(picture[0]).reshape(parts, shards, piece).transpose(1, 0, 2).reshape(total)
    pic_col, pic_row = pic[:, None], pic[None, :]
    vectors_own = jnp.stack([gain_one, shift_one, gain_two, shift_two, out_bias, down_bias])
    vectors_own = jnp.pad(vectors_own, ((0, EXTRA - vectors_own.shape[0]), (0, 0)))
    qkv_spans = tuple(
        tuple((s * width + f * rows, s * width + (f + 1) * rows) for s in range(3)) for f in range(shards)
    )
    up_spans = tuple(((f * units, (f + 1) * units),) for f in range(shards))
    up_near, core, far = call(
        functools.partial(cut_both_kernel, up_spans),
        [low_like(rows, units), low_like(2, rows, width), low_like(3, rows // 2, width)],
        (idx, up_weight, out_weight),
        [pltpu.VMEM((shards, rows, units), BF)],
        name="cut_up",
    )
    core, far = swap(core, "fsdp", 1), swap(far, "fsdp", 2)
    far_z = swap(far, "ctx", 1)
    far_core = swap(jnp.stack([far[1:], far_z[1:]]), "fsdp", 1)
    tokens_own, cot_own = share(patches[0], cotangent[0], after=(up_near,))
    qkv_parts = spread(
        *call(
            functools.partial(cut_kernel, qkv_spans),
            [low_like(rows + EXTRA, 3 * rows)] * 2 + [low_like(rows // 2 + EXTRA, 3 * rows)] * 2,
            (idx, qkv_weight, vectors_own),
            [pltpu.VMEM((shards, rows, 3 * rows), BF)],
            name="cut_qkv",
            after=(up_near,),
        )
    )
    token_parts = gather(tokens_own)

    cot_two = swap(cot_own, "fsdp", 2)
    cot_others = swap(jnp.concatenate([cot_own, cot_two], axis=0), "fsdp", 1)

    tokens, normed_one, qkv_own, vectors, queries, keys, values, mixed, logs = call(
        project_kernel,
        [
            low_like(total, width),
            low_like(total, width),
            low_like(width, 3 * rows),
            full_like(8, width),
            low_like(total, rows),
            low_like(total, rows),
            low_like(total, rows),
            low_like(total, rows),
            full_like(total, rows // HEAD_DIM),
        ],
        (idx, *token_parts, *qkv_parts, pic_col, pic_row, query_bias[None], value_bias[None]),
        [pltpu.VMEM((shards, 8, rows), F32)],
        name="project",
        us=10,
    )
    mixed_parts = gather(mixed)
    normed_two, activated, slope, up_own, attended_own = call(
        unit_kernel,
        [
            low_like(total, width),
            low_like(total, units),
            full_like(total, units),
            low_like(width, units),
            full_like(seg, width),
        ],
        (
            idx, tokens, *mixed_parts, out_weight, vectors, up_near, core, far, far_z, far_core, up_bias[None],
        ),
        [pltpu.VMEM((total, width), BF), pltpu.VMEM((width, width), BF), pltpu.VMEM((total, width), F32)],
        name="units",
        us=12,
    )
    hidden_grad, cot, up_bias_grad = call(
        unit_back_kernel,
        [low_like(total, units), low_like(total, width), full_like(1, units)],
        (idx, cot_own, cot_two, cot_others, slope, down_weight),
        name="unit_back",
        us=5,
    )

    padded = (units + 63) // 64 * 64
    sums = {}
    last_steps = [(axis, 2**i) for axis, size in (("rep", reps), ("ctx", parts)) for i in range(1, size.bit_length() - 1)]

    def swap_both(value):
        pairs = [(r * parts + c, (r ^ 1) * parts + (c ^ 1)) for r in range(reps) for c in range(parts)]
        return lax.ppermute(value, ("rep", "ctx"), pairs)

    def last_sums(value):
        for axis, bit in last_steps[:-1]:
            (value,) = call(sum_kernel, [low_like(*value.shape)], (idx, value, swap(value, axis, bit)), name="more")
        return value, swap(value, *last_steps[-1])

    def step(name, number, after):
        run = functools.partial(call, after=after, name=f"{name}_{number}")
        keep, *got = sums[name]
        if number == 1:
            value, send = run(halve_kernel, [low_like(*keep.shape[1:])] * 2, (idx, keep, *got))
            sums[name] = value, swap(send, "ctx", 1)
        elif number == 2:
            (value,) = run(sum_kernel, [low_like(*keep.shape)], (idx, keep, *got))
            sums[name] = last_sums(value)
        elif number == 3 and name == "d":
            (value,) = run(sum_kernel, [low_like(*keep.shape)], (idx, keep, *got))
            sums[name] = value, swap(value, "ctx", 1)
        elif name != "d" and number == 3:
            outs = [low_like(rows // 4, keep.shape[1])] * shards
            if name == "q":
                outs += [low_like(rows // 3, keep.shape[1]), full_like(EXTRA, keep.shape[1])]
            outs = list(run(functools.partial(deal_kernel, shards), outs, (idx, keep, *got)))
            value = outs[0]
            sums[name] = [value] + [swap(outs[bit], "fsdp", bit) for bit in range(1, shards)] + outs[shards : shards + 1]
            if name == "q":
                val["lines"] = outs[shards + 1]
        elif name != "d" and number == 4:
            blocks = sums[name]
            total_rows = sum(part.shape[0] for part in blocks)
            (value,) = run(
                functools.partial(join_kernel, shards), [low_like(total_rows, keep.shape[1])], (idx, *blocks)
            )
            if name == "q":
                sums[name] = value, swap(value, "rep", 1), swap(value, "ctx", 1), swap_both(value)
            else:
                sums[name] = value, swap(value, "ctx", 1)
        else:
            (value,) = run(stack_kernel, [low_like(2, *keep.shape)], (idx, keep, *got))
            sums[name] = value, swap(value, "rep", 1)
        return value

    qkv_places = tuple(
        tuple((s * rows, (s + 1) * rows, s * width + f * rows) for s in range(3)) for f in range(shards)
    )
    val = {}
    cut = lambda full: lax.dynamic_slice_in_dim(full, own * rows, rows, 1)
    shared = [full_like(2 * seg, width), low_like(2 * seg, width)]

    def run_unit_grads(after):
        down_keep, down_send, up_keep, up_send, val["cot_sum"] = call(
            unit_grads_kernel,
            [low_like(2, padded // 4, width)] * 2 + [low_like(2, rows, units)] * 2 + [full_like(1, width)],
            (idx, activated, cot, normed_two, hidden_grad),
            [pltpu.VMEM((padded, width), F32), pltpu.VMEM((width, units), F32)],
            name="unit_grads",
        us=8,
            after=after,
        )
        sums["d"] = down_keep, swap(down_send, "rep", 1)
        sums["u"] = up_keep, swap(up_send, "rep", 1)
        return val["cot_sum"]

    def run_norm_two_grad(after):
        keep, send = call(
            norm_grad_kernel,
            shared,
            (idx, hidden_grad, up_own),
            [pltpu.VMEM((total, width), F32)],
            name="norm_two_grad",
        us=4,
            after=after,
        )
        val["two"] = keep, swap(send, "fsdp", 1)
        return keep

    def run_branch(after):
        keep, send = call(
            branch_kernel,
            shared,
            (idx, activated, down_weight),
            [pltpu.VMEM((total, width), F32)],
            name="branch",
        us=4,
            after=after,
        )
        val["out"] = keep, swap(send, "fsdp", 1)
        return keep

    def run_add(key, after):
        near, onward = call(
            add_kernel,
            [full_like(seg, width), low_like(seg, width)],
            (idx, *val[key]),
            name="add_" + key,
            after=after,
        )
        val[key] = near, swap(onward, "fsdp", 2)
        return near

    def run_norm_two_back(after):
        val["attended_grad"], low_grad, val["sums_two"] = call(
            functools.partial(norm_back_kernel, 2),
            [full_like(seg, width), low_like(seg, width), full_like(2, width)],
            (idx, *val["two"], attended_own, cot_own, vectors),
            name="norm_two_back",
            after=after,
        )
        val["branch_grad"] = gather(low_grad)
        return val["sums_two"]

    def run_attend_back(after):
        val["branch_grad"], val["projected_grad"], val["sum_q"], val["sum_v"], val["branch_sum"] = call(
            attend_back_kernel,
            [
                low_like(total, width),
                low_like(total, 3 * rows),
                full_like(1, rows),
                full_like(1, rows),
                full_like(1, width),
            ],
            (idx, *val["branch_grad"], out_weight, pic_col, pic_row, queries, keys, values, logs),
            [pltpu.VMEM((total, rows), BF)],
            name="attend_back",
        us=9,
            after=after,
        )
        return val["sum_q"]

    def run_qkv_grads(after):
        names = ("sum_q", "sum_v", "branch_sum", "cot_sum")
        keep, send = call(
            qkv_grads_kernel,
            [low_like(2, rows + rows // 3 + EXTRA, 3 * rows)] * 2,
            (
                idx, normed_one, val["projected_grad"], mixed, val["branch_grad"], *(val[name] for name in names),
                up_bias_grad, val["sums_one"], val["sums_two"],
            ),
            [pltpu.VMEM((width, 3 * rows), F32), pltpu.VMEM((rows, width), F32), pltpu.VMEM((EXTRA, 3 * rows), F32)],
            name="qkv_grads",
        us=5,
            after=after,
        )
        sums["q"] = keep, swap(send, "rep", 1)
        return keep

    def run_norm_one_grad(after):
        keep, send, val["sums_one"] = call(
            norm_grad_sums_kernel,
            shared + [full_like(2, width)],
            (idx, val["projected_grad"], qkv_own, tokens),
            [pltpu.VMEM((total, width), F32)],
            name="norm_one_grad",
        us=4,
            after=after,
        )
        val["one"] = keep, swap(send, "fsdp", 1)
        return keep

    def run_norm_one_back(after):
        low_grad, _ = call(
            functools.partial(norm_back_kernel, 0),
            [low_like(seg, width), full_like(2, width)],
            (idx, *val["one"], tokens_own, val["attended_grad"], vectors),
            name="norm_one_back",
            after=after,
        )
        val["input_grad"] = low_grad
        return low_grad

    def run_output(after):
        (low,) = call(
            output_kernel, [low_like(seg, width)], (idx, *val["out"], attended_own, vectors), name="output", after=after
        )
        val["output"] = low
        return low

    def run_lines(number, after):
        if number > 1:
            (val["lines"],) = call(
                total_kernel,
                [full_like(*val["lines"].shape)],
                (idx, *val["lines_parts"]),
                name=f"lines_{number}",
                after=after,
            )
        else:
            val["own_lines"] = val["lines"]
        if number < 3:
            val["lines_parts"] = val["lines"], swap(val["lines"], "fsdp", number)
        return val["lines"]

    def run_share_back(after):
        val["shared"] = share_back(val["output"], val["input_grad"])
        return after[0]

    def run_outputs(after):
        outs = call(
            part_tokens_kernel, [low_like(shards, piece, width)] * 2, (idx, val["shared"]), name="outs", after=after
        )
        val["output"], val["input_grad"] = (value.reshape(seg, width) for value in outs)
        return outs[0]

    def run_place(key, after):
        run = functools.partial(call, name="place_" + key, after=after)
        if key == "d":
            (val["d"],) = run(place_down_kernel, [full_like(units, width)], (idx, *sums["d"]))
        elif key == "u":
            (val["u"],) = run(place_up_kernel, [full_like(rows, shards * units)], (idx, *sums["u"]))
        else:
            outs = [full_like(rows, 3 * width), full_like(rows, width)]
            val["q"], val["o"] = run(functools.partial(place_qkv_kernel, qkv_places), outs, (idx, *sums["q"]))
        return val[key]

    tasks = {
        "ugrads": run_unit_grads,
        "ng2": run_norm_two_grad,
        "br": run_branch,
        "add2": functools.partial(run_add, "two"),
        "addo": functools.partial(run_add, "out"),
        "add1": functools.partial(run_add, "one"),
        "K3": run_norm_two_back,
        "K4": run_attend_back,
        "K5": run_norm_one_back,
        "fin": run_output,
        "back": run_share_back,
        "outs": run_outputs,
        "qg": run_qkv_grads,
        "ng1": run_norm_one_grad,
    }
    token = (hidden_grad,)
    for name in SCHEDULE:
        if name in tasks:
            token = (tasks[name](token),)
        elif name.startswith("place_"):
            token = (run_place(name[6:], token),)
        elif name.startswith("v"):
            token = (run_lines(int(name[1:]), token),)
        else:
            token = (step(name[:-1], int(name[-1]), token),)
    lines, own_lines = val["lines"], val["own_lines"]
    vector_of = lambda i: own_lines[i // 3, i % 3 * rows : (i % 3 + 1) * rows]
    norms = jnp.concatenate([lines[4:12:2], lines[5:12:2, :rows]], axis=1)
    norms = lax.dynamic_slice_in_dim(norms, own * rows, rows, 1)
    return (
        val["output"][None],
        val["input_grad"][None],
        norms[0],
        norms[1],
        val["q"],
        vector_of(0),
        vector_of(1),
        val["o"],
        vector_of(2),
        norms[2],
        norms[3],
        val["u"],
        own_lines[2:4].reshape(-1)[:units],
        val["d"],
        vector_of(3),
    )


def solution(mesh):
    sizes = tuple(mesh.shape[axis] for axis in ("rep", "fsdp", "ctx"))
    tokens = P(("rep", "fsdp"), "ctx", None)
    vector, matrix = P("fsdp"), P("fsdp", None)
    return jax.shard_map(
        functools.partial(per_device, sizes),
        mesh=mesh,
        in_specs=(
            tokens,
            P(("rep", "fsdp"), None),
            vector,
            vector,
            matrix,
            vector,
            vector,
            matrix,
            vector,
            vector,
            vector,
            matrix,
            vector,
            matrix,
            vector,
            tokens,
        ),
        out_specs=(
            tokens,
            tokens,
            vector,
            vector,
            matrix,
            vector,
            vector,
            matrix,
            vector,
            vector,
            vector,
            matrix,
            vector,
            matrix,
            vector,
        ),
        check_vma=False,
    )
```

```python
import functools

import jax
import jax.numpy as jnp
from jax import lax
from jax.experimental import pallas as pl
from jax.experimental.pallas import tpu as pltpu
from jax.sharding import PartitionSpec as P

HEADS = 16
HEAD_DIM = 72
PICS = 3

EPSILON = 1e-06
MASKED = -1e30
BF = jnp.bfloat16
F32 = jnp.float32
SCALING = HEAD_DIM ** (-0.5)
TANH_SCALE = (2.0 / jnp.pi) ** 0.5
CUBIC = 0.044715
VMEM_LIMIT = 28 * 2**20
ORDER = (0, 2, 1, 3)
SCHEDULE = (
    "ng2", "ugrads", "add2", "br", "K3", "d1", "K4", "addo", "ng1", "d2", "qg", "u1", "add1", "d3", "fin",
    "u2", "K5", "d4", "q1", "u3", "q2", "u4", "back", "u5", "place_d", "q3", "q4", "v1", "place_u", "v2",
    "v3", "outs", "place_q",
)
EXTRA = 16


def dot(left, right):
    return jnp.dot(left, right, preferred_element_type=F32)


def dot_t(left, right):
    return lax.dot_general(left, right, (((1,), (1,)), ((), ())), preferred_element_type=F32)


def t_dot(left, right):
    return lax.dot_general(left, right, (((0,), (0,)), ((), ())), preferred_element_type=F32)


def rows_at(index, size):
    return pl.ds(pl.multiple_of(index * size, 8), size)


def norm_parts(values):
    center = values - jnp.mean(values, axis=-1, keepdims=True)
    spread = jnp.mean(center * center, axis=-1, keepdims=True)
    scale = lax.rsqrt(spread + EPSILON)
    return center * scale, scale


def norm_back(grad, normal, scale, gain):
    through = grad * gain
    mean_one = jnp.mean(through, axis=-1, keepdims=True)
    mean_two = jnp.mean(through * normal, axis=-1, keepdims=True)
    back = scale * (through - mean_one - normal * mean_two)
    return back, jnp.sum(grad * normal, axis=0, keepdims=True), jnp.sum(grad, axis=0, keepdims=True)


def call(kernel, outs, ins, scratch=(), name=None, after=(), us=1):
    vmem = pl.BlockSpec(memory_space=pltpu.VMEM)
    skip = len(after)

    def body(*refs):
        kernel(*refs[skip:])

    return pl.pallas_call(
        body,
        out_shape=outs,
        in_specs=[pl.BlockSpec(memory_space=pl.ANY)] * skip
        + [pl.BlockSpec(memory_space=pltpu.SMEM)]
        + [vmem] * (len(ins) - 1),
        out_specs=[vmem] * len(outs),
        scratch_shapes=list(scratch),
        compiler_params=pltpu.CompilerParams(vmem_limit_bytes=VMEM_LIMIT),
        cost_estimate=pl.CostEstimate(flops=us * 10**9, bytes_accessed=0, transcendentals=0),
        name=name,
    )(*after, *ins)


def low_like(*shape):
    return jax.ShapeDtypeStruct(shape, BF)


def full_like(*shape):
    return jax.ShapeDtypeStruct(shape, F32)


def cut_columns(spans, weight, stack):
    for f, parts in enumerate(spans):
        place = 0
        for start, stop in parts:
            stack[f, :, place : place + stop - start] = weight[:, start:stop]
            place += stop - start


def cut_kernel(spans, idx, weight, vectors, near, core, far_two, far_three, stack):
    rows = weight.shape[0]
    own, low = idx[0], idx[1]
    cut_columns(spans, weight, stack)
    for bit, out in enumerate((near, core, far_two, far_three)):
        size = out.shape[0] - EXTRA
        out[:size] = stack[own ^ bit] if size == rows else stack[own ^ bit, rows_at(low, size)]
        out[size:] = jnp.zeros((EXTRA, out.shape[1]), BF)
        out[size:, : vectors.shape[1]] = vectors[...]


def cut_both_kernel(spans, idx, weight, out_weight, near, core, far, stack):
    own, low = idx[0], idx[2]
    half = weight.shape[0] // 2
    columns = weight.shape[1] // len(spans)
    cut_columns(spans, weight, stack)
    near[...] = stack[own]
    core[0, :, :columns] = stack[own ^ 1]
    core[1] = out_weight[...]
    far[0, :, :columns] = stack[own ^ 2, rows_at(low, half)]
    far[1, :, :columns] = stack[own ^ 3, rows_at(low, half)]
    far[2] = out_weight[rows_at(low, half)]


def place_halves(low, target, block, mine, other):
    half = mine.shape[0]
    target[rows_at(2 * block + low, half)] = mine
    target[rows_at(2 * block + 1 - low, half)] = other


def pair_kernel(idx, first, second, out):
    out[: first.shape[0]] = first[...]
    out[first.shape[0] :] = second[...]


def join_tokens_kernel(idx, *refs):
    for i, ref in enumerate(refs[:-1]):
        for f in range(ref.shape[0]):
            refs[-1][f, i] = ref[f]


def part_tokens_kernel(idx, source, *outs):
    for i, out in enumerate(outs):
        for c in range(out.shape[0]):
            out[c] = source[c, i]


def allowed_of(pic_col, pic_row):
    total = pic_row.shape[1]
    rows = lax.broadcasted_iota(jnp.int32, (total, total), 0)
    columns = lax.broadcasted_iota(jnp.int32, (total, total), 1)
    return (pic_col == pic_row) & ((pic_row != PICS) | (rows == columns))


def project_kernel(
    idx, tok_0, tok_2, tok_1, tok_3, near, core, far_two, far_two_y, far_three, far_three_y, pic_col, pic_row, query_bias, value_bias,
    tokens, normed, weight, vectors, queries, keys, values, mixed, logs, pieces,
):
    own = idx[0]
    rows = queries.shape[1]
    block = tok_0.shape[0]
    half = rows // 2
    weight[rows_at(own, rows)] = near[:rows]
    weight[rows_at(own ^ 1, rows)] = core[:rows]
    place_halves(idx[1], weight, own ^ 2, far_two[:half], far_two_y[:half])
    place_halves(idx[1], weight, own ^ 3, far_three[:half], far_three_y[:half])
    for bit, ref in enumerate((near, core, far_two, far_three)):
        pieces[bit] = ref[ref.shape[0] - EXTRA :, :rows].astype(F32)[:8]
    vectors[...] = jnp.concatenate([pieces[own ^ f] for f in range(len(ORDER))], axis=1)
    gain, shift = vectors[0:1], vectors[1:2]
    for bit, ref in zip(ORDER, (tok_0, tok_2, tok_1, tok_3)):
        part = ref[...]
        tokens[rows_at(own ^ bit, block)] = part
        normed[rows_at(own ^ bit, block)] = (norm_parts(part.astype(F32))[0] * gain + shift).astype(BF)
    query_add, value_add = query_bias[...].astype(F32), value_bias[...].astype(F32)

    result = dot(normed[...], weight[...])
    queries[...] = (SCALING * (result[:, :rows] + query_add)).astype(BF)
    keys[...] = result[:, rows : 2 * rows].astype(BF)
    values[...] = (result[:, 2 * rows :] + value_add).astype(BF)
    allowed = allowed_of(pic_col[...], pic_row[...])
    outs, log_parts = [], []
    for h in range(rows // HEAD_DIM):
        cut = slice(h * HEAD_DIM, (h + 1) * HEAD_DIM)
        scores = jnp.where(allowed, dot_t(queries[:, cut], keys[:, cut]), MASKED)
        largest = jnp.max(scores, axis=-1, keepdims=True)
        expo = jnp.exp(scores - largest)
        sums = jnp.sum(expo, axis=-1, keepdims=True)
        probs = (expo * (1.0 / sums)).astype(BF)
        outs.append(dot(probs, values[:, cut]))
        log_parts.append(largest + jnp.log(sums))
    mixed[...] = jnp.concatenate(outs, axis=1).astype(BF)
    logs[...] = jnp.concatenate(log_parts, axis=1)


def unit_kernel(
    idx, tokens, mix_0, mix_2, mix_1, mix_3, out_0, vectors, near, core, far, far_z, far_core, up_bias,
    normed, activated, slope, up, attended_own, mix, out, attended,
):
    own = idx[0]
    rows, columns, block = mix_0.shape[1], near.shape[1], attended_own.shape[0]
    up[rows_at(own, rows)] = near[...]
    up[rows_at(own ^ 1, rows)] = core[0, :, :columns]
    place_halves(idx[2], up, own ^ 2, far[0, :, :columns], far_z[0, :, :columns])
    place_halves(idx[2], up, own ^ 3, far_core[0, 0, :, :columns], far_core[1, 0, :, :columns])
    for place, ref in enumerate((mix_0, mix_2, mix_1, mix_3)):
        mix[:, place * rows : (place + 1) * rows] = ref[...]
    out[:rows] = out_0[...]
    place_halves(idx[2], out, 1, far[2], far_z[2])
    out[2 * rows : 3 * rows] = core[1]
    place_halves(idx[2], out, 3, far_core[0, 1], far_core[1, 1])
    gain, shift, out_shift = vectors[2:3], vectors[3:4], vectors[4:5]
    stream = tokens[...].astype(F32) + dot(mix[...], out[...]) + out_shift
    attended[...] = stream
    normed[...] = (norm_parts(stream)[0] * gain + shift).astype(BF)
    hidden = dot(normed[...], up[...]) + up_bias[...].astype(F32)
    square = hidden * hidden
    tanh = jnp.tanh(TANH_SCALE * hidden * (1.0 + CUBIC * square))
    activated[...] = (0.5 * hidden * (1.0 + tanh)).astype(BF)
    slope[...] = 0.5 * (1.0 + tanh) + 0.5 * hidden * (1.0 - tanh * tanh) * (
        TANH_SCALE * (1.0 + 3.0 * CUBIC * square)
    )
    attended_own[...] = attended[rows_at(own, block)]


def unit_back_kernel(idx, cot_0, cot_2, cot_13, slope, down, hidden_grad, cot, bias_grad):
    own = idx[0]
    block = cot_0.shape[0]
    for bit, part in ((0, cot_0[...]), (2, cot_2[...]), (1, cot_13[:block]), (3, cot_13[block:])):
        cot[rows_at(own ^ bit, block)] = part
    grad = (dot_t(cot[...], down[...]) * slope[...]).astype(BF)
    hidden_grad[...] = grad
    bias_grad[...] = jnp.sum(grad.astype(F32), axis=0, keepdims=True)


def parts_of_rows(idx, part, keep, send):
    own = idx[0]
    block = keep.shape[0] // 2
    for place, bit in ((0, 0), (1, 2)):
        keep[place * block : (place + 1) * block] = part[rows_at(own ^ bit, block)]
    for place, bit in ((0, 1), (1, 3)):
        send[place * block : (place + 1) * block] = part[rows_at(own ^ bit, block)].astype(BF)


def norm_grad_kernel(idx, grad, weight, keep, send, part):
    part[...] = dot_t(grad[...], weight[...])
    parts_of_rows(idx, part, keep, send)


def norm_grad_sums_kernel(idx, grad, weight, tokens, keep, send, sums, part):
    result = dot_t(grad[...], weight[...])
    part[...] = result
    parts_of_rows(idx, part, keep, send)
    normal = norm_parts(tokens[...].astype(F32))[0]
    sums[0:1] = jnp.sum(result * normal, axis=0, keepdims=True)
    sums[1:2] = jnp.sum(result, axis=0, keepdims=True)


def total_kernel(idx, left, right, out):
    out[...] = left[...] + right[...]


def branch_kernel(idx, activated, down, keep, send, part):
    part[...] = dot(activated[...], down[...])
    parts_of_rows(idx, part, keep, send)


def split_rows(idx, source, groups, keep, send):
    low = idx[1]
    size = keep.shape[1] // groups
    for out, outer in ((keep, low), (send, 1 - low)):
        for half in range(2):
            for g in range(groups):
                piece = source[rows_at(4 * g + 2 * outer + half, size)]
                out[half, g * size : (g + 1) * size] = piece.astype(BF)


def unit_grads_kernel(
    idx, activated, cot, normed, hidden_grad, down_keep, down_send, up_keep, up_send, cot_sum, down_grad, up_grad
):
    units = activated.shape[1]
    down_grad[units // 8 * 8 :] = jnp.zeros((down_grad.shape[0] - units // 8 * 8, down_grad.shape[1]), F32)
    down_grad[:units] = t_dot(activated[...], cot[...])
    split_rows(idx, down_grad, 1, down_keep, down_send)
    up_grad[...] = t_dot(normed[...], hidden_grad[...])
    split_rows(idx, up_grad, 4, up_keep, up_send)
    cot_sum[...] = jnp.sum(cot[...].astype(F32), axis=0, keepdims=True)


def add_kernel(idx, keep, got, near, send):
    block = near.shape[0]
    near[...] = keep[:block] + got[:block].astype(F32)
    send[...] = (keep[block:] + got[block:].astype(F32)).astype(BF)


def output_kernel(idx, near, got, attended, vectors, out):
    out[...] = (attended[...] + near[...] + got[...].astype(F32) + vectors[5:6]).astype(BF)


def norm_back_kernel(row, idx, near, got, source, add, vectors, *outs):
    *grad, low_grad, sums = outs
    grad_in = near[...] + got[...].astype(F32)
    normal, scale = norm_parts(source[...].astype(F32))
    back, gain_sum, shift_sum = norm_back(grad_in, normal, scale, vectors[row : row + 1])
    result = add[...].astype(F32) + back
    for out in grad:
        out[...] = result
    low_grad[...] = result.astype(BF)
    sums[...] = jnp.concatenate([gain_sum, shift_sum], axis=0)


def attend_back_kernel(
    idx, grad_0, grad_2, grad_1, grad_3, out_weight, pic_col, pic_row, queries, keys, values, logs,
    branch_grad, projected_grad, sum_q, sum_v, branch_sum, mixed_grad,
):
    own = idx[0]
    block, rows = grad_0.shape[0], queries.shape[1]
    for bit, ref in zip(ORDER, (grad_0, grad_2, grad_1, grad_3)):
        branch_grad[rows_at(own ^ bit, block)] = ref[...]
    branch_sum[...] = jnp.sum(branch_grad[...].astype(F32), axis=0, keepdims=True)
    mixed_grad[...] = dot_t(branch_grad[...], out_weight[...]).astype(BF)
    allowed = allowed_of(pic_col[...], pic_row[...])
    query_parts, key_parts, value_parts = [], [], []
    for h in range(rows // HEAD_DIM):
        cut = slice(h * HEAD_DIM, (h + 1) * HEAD_DIM)
        query, key, value, grad = queries[:, cut], keys[:, cut], values[:, cut], mixed_grad[:, cut]
        scores = jnp.where(allowed, dot_t(query, key), MASKED)
        probs = jnp.exp(scores - logs[:, h : h + 1])
        probs_grad = dot_t(grad, value)
        delta = jnp.sum(probs * probs_grad, axis=-1, keepdims=True)
        scores_grad = (probs * (probs_grad - delta)).astype(BF)
        query_parts.append(dot(scores_grad, key))
        key_parts.append(t_dot(scores_grad, query))
        value_parts.append(t_dot(probs.astype(BF), grad))
    query_grad = SCALING * jnp.concatenate(query_parts, axis=1)
    value_grad = jnp.concatenate(value_parts, axis=1)
    projected_grad[:, :rows] = query_grad.astype(BF)
    projected_grad[:, rows : 2 * rows] = jnp.concatenate(key_parts, axis=1).astype(BF)
    projected_grad[:, 2 * rows :] = value_grad.astype(BF)
    sum_q[...] = jnp.sum(query_grad, axis=0, keepdims=True)
    sum_v[...] = jnp.sum(value_grad, axis=0, keepdims=True)


def fold(piece, columns):
    size = piece.shape[0] // 3
    rest = [piece[i * size : (i + 1) * size, columns:] for i in range(3)]
    return piece[:, :columns], jnp.concatenate(rest, axis=1)


def quarter_places(idx):
    rep, ctx = idx[1], idx[2]
    return 2 * rep + ctx, 2 * (1 - rep) + ctx, 2 * rep + 1 - ctx, 2 * (1 - rep) + 1 - ctx


def qkv_grads_kernel(
    idx, normed, projected_grad, mixed, branch_grad, sum_q, sum_v, branch_sum, cot_sum, bias_grad, sums_one, sums_two,
    keep, send, grad, out_grad, lines,
):
    rows, columns, units = sum_q.shape[1], grad.shape[1], bias_grad.shape[1]
    grad[...] = t_dot(normed[...], projected_grad[...])
    out_grad[...] = t_dot(mixed[...], branch_grad[...])

    def quarter(row):
        parts = [row[:, f * rows : (f + 1) * rows] for f in range(grad.shape[0] // rows)]
        return sum(jnp.where(idx[0] == f, part, 0.0) for f, part in enumerate(parts))

    lines[...] = jnp.zeros_like(lines)
    vectors = [sum_q[...], sum_v[...], quarter(branch_sum[...]), quarter(cot_sum[...])]
    for i, vector in enumerate(vectors):
        lines[i // 3 : i // 3 + 1, i % 3 * rows : (i % 3 + 1) * rows] = vector
    lines[2:3] = bias_grad[:, :columns]
    lines[3:4, : units - columns] = bias_grad[:, columns:]
    for i, ref in enumerate((sums_one, sums_two)):
        for j in range(2):
            at = 4 + 4 * i + 2 * j
            lines[at : at + 1] = ref[j : j + 1, :columns]
            lines[at + 1 : at + 2, :rows] = ref[j : j + 1, columns:]
    size = rows // 4
    place = grad.shape[0] // 4
    for out, outer in ((keep, idx[1]), (send, 1 - idx[1])):
        for half in range(2):
            for g in range(grad.shape[0] // rows):
                piece = grad[rows_at(4 * g + 2 * outer + half, size)]
                out[half, g * size : (g + 1) * size] = piece.astype(BF)
            upper, lower = fold(out_grad[rows_at(2 * outer + half, size)], columns)
            out[half, place : place + size] = upper.astype(BF)
            out[half, place + size : place + size + size // 3] = lower.astype(BF)
            out[half, place + size + size // 3 :] = lines[...].astype(BF)


def add_low(left, right):
    return left.astype(F32) + right.astype(F32)


def halve_kernel(idx, keep, got, keep_next, send):
    low = idx[2]
    keep_next[...] = add_low(keep[low], got[low]).astype(BF)
    send[...] = add_low(keep[1 - low], got[1 - low]).astype(BF)


def sum_kernel(idx, keep, got, out):
    out[...] = add_low(keep[...], got[...]).astype(BF)


def deal_kernel(groups, idx, keep, got, *outs):
    size = outs[0].shape[0]
    for bit in range(groups):
        cut = rows_at(idx[0] ^ bit, size)
        outs[bit][...] = add_low(keep[cut], got[cut]).astype(BF)
    place = groups * size
    for ref in outs[groups:]:
        cut = slice(place, place + ref.shape[0])
        ref[...] = add_low(keep[cut], got[cut]).astype(ref.dtype)
        place += ref.shape[0]


def join_kernel(groups, idx, *refs):
    out = refs[-1]
    size = refs[0].shape[0]
    for bit in range(groups):
        out[rows_at(idx[0] ^ bit, size)] = refs[bit][...]
    for ref in refs[groups:-1]:
        out[groups * size :] = ref[...]


def stack_kernel(idx, mine, got, out):
    out[0] = mine[...]
    out[1] = got[...]


def quarters_of(idx, mine, got):
    for outer, ref in ((idx[1], mine), (1 - idx[1], got)):
        for rel in range(2):
            inner = idx[2] if rel == 0 else 1 - idx[2]
            yield 2 * outer + inner, ref.at[rel]


def place_down_kernel(idx, mine, got, out):
    size, total = mine.shape[1], out.shape[0]
    for quarter, piece in quarters_of(idx, mine, got):

        @pl.when(quarter < 3)
        def _(quarter=quarter, piece=piece):
            out[rows_at(quarter, size)] = piece[...].astype(F32)

        @pl.when(quarter == 3)
        def _(piece=piece):
            out[3 * size :] = piece[...].astype(F32)[: total - 3 * size]


def place_up_kernel(idx, mine, got, out):
    size, columns = out.shape[0] // 4, mine.shape[2]
    for quarter, piece in quarters_of(idx, mine, got):
        for f in range(out.shape[1] // columns):
            block = piece[f * size : (f + 1) * size].astype(F32)
            out[rows_at(quarter, size), f * columns : (f + 1) * columns] = block


def place_qkv_kernel(spans, idx, own, from_rep, from_ctx, from_both, out, out_out):
    size = out.shape[0] // 4
    columns = own.shape[1]
    place = len(spans) * size
    width = out_out.shape[1] - columns
    for quarter, piece in zip(quarter_places(idx), (own, from_rep, from_ctx, from_both)):
        at = rows_at(quarter, size)
        for f, parts in enumerate(spans):
            block = piece[f * size : (f + 1) * size].astype(F32)
            for start, stop, target in parts:
                out[at, target : target + stop - start] = block[:, start:stop]
        out_out[at, :columns] = piece[place : place + size].astype(F32)
        rest = piece[place + size :].astype(F32)
        rest = jnp.concatenate([rest[:, i * width : (i + 1) * width] for i in range(3)], axis=0)
        out_out[at, columns:] = rest


def per_device(
    sizes,
    patches,
    picture,
    gain_one,
    shift_one,
    qkv_weight,
    query_bias,
    value_bias,
    out_weight,
    out_bias,
    gain_two,
    shift_two,
    up_weight,
    up_bias,
    down_weight,
    down_bias,
    cotangent,
):
    reps, shards, parts = sizes
    own = lax.axis_index("fsdp")
    low_rep, low_ctx = lax.rem(lax.axis_index("rep"), 2), lax.rem(lax.axis_index("ctx"), 2)
    idx = jnp.stack([own, low_rep, low_ctx, lax.axis_index("ctx")]).astype(jnp.int32)
    seg, width = patches.shape[1], patches.shape[2]
    total = picture.shape[1]
    rows = width // shards
    units = up_bias.shape[0]

    def swap(value, axis, bit):
        size = {"rep": reps, "fsdp": shards, "ctx": parts}[axis]
        return lax.ppermute(value, axis, [(i, i ^ bit) for i in range(size)])

    def turn(value):
        pairs = [(f * parts + c, c * parts + f) for f in range(shards) for c in range(parts)]
        return lax.ppermute(value, ("fsdp", "ctx"), pairs)

    def gather(value):
        far = swap(value, "fsdp", 2)
        return value, far, swap(value, "fsdp", 1), swap(far, "fsdp", 1)

    def scatter(keep, send, name, after=()):
        near, onward = call(
            add_kernel,
            [full_like(seg, width), low_like(seg, width)],
            (idx, keep, swap(send, "fsdp", 1)),
            name=name,
            after=after,
        )
        return near, swap(onward, "fsdp", 2)

    piece = seg // shards

    def share(*values, after):
        (value,) = call(
            join_tokens_kernel,
            [low_like(shards, len(values), piece, width)],
            (idx, *(value.reshape(shards, piece, width) for value in values)),
            name="join_tokens",
            after=after,
        )
        value = lax.all_to_all(lax.all_to_all(value, "fsdp", 0, 0), "ctx", 0, 0)
        parted = call(part_tokens_kernel, [low_like(parts, piece, width)] * len(values), (idx, value), name="part_tokens")
        return [value.reshape(seg, width) for value in parted]

    def share_back(*values):
        value = jnp.stack([value.reshape(parts, piece, width) for value in values], axis=1)
        return lax.all_to_all(lax.all_to_all(value, "ctx", 0, 0), "fsdp", 0, 0)

    def spread(near, core, far_two, far_three):
        far_two, far_three = swap(far_two, "fsdp", 2), swap(far_three, "fsdp", 3)
        return near, swap(core, "fsdp", 1), far_two, swap(far_two, "rep", 1), far_three, swap(far_three, "rep", 1)

    pic = turn(picture[0]).reshape(parts, shards, piece).transpose(1, 0, 2).reshape(total)
    pic_col, pic_row = pic[:, None], pic[None, :]
    vectors_own = jnp.stack([gain_one, shift_one, gain_two, shift_two, out_bias, down_bias])
    vectors_own = jnp.pad(vectors_own, ((0, EXTRA - vectors_own.shape[0]), (0, 0)))
    qkv_spans = tuple(
        tuple((s * width + f * rows, s * width + (f + 1) * rows) for s in range(3)) for f in range(shards)
    )
    up_spans = tuple(((f * units, (f + 1) * units),) for f in range(shards))
    up_near, core, far = call(
        functools.partial(cut_both_kernel, up_spans),
        [low_like(rows, units), low_like(2, rows, width), low_like(3, rows // 2, width)],
        (idx, up_weight, out_weight),
        [pltpu.VMEM((shards, rows, units), BF)],
        name="cut_up",
    )
    core, far = swap(core, "fsdp", 1), swap(far, "fsdp", 2)
    far_z = swap(far, "ctx", 1)
    far_core = swap(jnp.stack([far[1:], far_z[1:]]), "fsdp", 1)
    tokens_own, cot_own = share(patches[0], cotangent[0], after=(up_near,))
    qkv_parts = spread(
        *call(
            functools.partial(cut_kernel, qkv_spans),
            [low_like(rows + EXTRA, 3 * rows)] * 2 + [low_like(rows // 2 + EXTRA, 3 * rows)] * 2,
            (idx, qkv_weight, vectors_own),
            [pltpu.VMEM((shards, rows, 3 * rows), BF)],
            name="cut_qkv",
            after=(up_near,),
        )
    )
    token_parts = gather(tokens_own)


    tokens, normed_one, qkv_own, vectors, queries, keys, values, mixed, logs = call(
        project_kernel,
        [
            low_like(total, width),
            low_like(total, width),
            low_like(width, 3 * rows),
            full_like(8, width),
            low_like(total, rows),
            low_like(total, rows),
            low_like(total, rows),
            low_like(total, rows),
            full_like(total, rows // HEAD_DIM),
        ],
        (idx, *token_parts, *qkv_parts, pic_col, pic_row, query_bias[None], value_bias[None]),
        [pltpu.VMEM((shards, 8, rows), F32)],
        name="project",
        us=10,
    )
    cot_two = swap(cot_own, "fsdp", 2)
    mixed_parts = gather(mixed)
    normed_two, activated, slope, up_own, attended_own = call(
        unit_kernel,
        [
            low_like(total, width),
            low_like(total, units),
            full_like(total, units),
            low_like(width, units),
            full_like(seg, width),
        ],
        (
            idx, tokens, *mixed_parts, out_weight, vectors, up_near, core, far, far_z, far_core, up_bias[None],
        ),
        [pltpu.VMEM((total, width), BF), pltpu.VMEM((width, width), BF), pltpu.VMEM((total, width), F32)],
        name="units",
        us=12,
    )
    (cot_pair,) = call(
        pair_kernel, [low_like(2 * seg, width)], (idx, cot_own, cot_two), name="pair_cot", after=(activated,)
    )
    cot_others = swap(cot_pair, "fsdp", 1)
    hidden_grad, cot, up_bias_grad = call(
        unit_back_kernel,
        [low_like(total, units), low_like(total, width), full_like(1, units)],
        (idx, cot_own, cot_two, cot_others, slope, down_weight),
        name="unit_back",
        us=5,
    )

    padded = (units + 63) // 64 * 64
    sums = {}
    last_steps = [(axis, 2**i) for axis, size in (("rep", reps), ("ctx", parts)) for i in range(1, size.bit_length() - 1)]

    def swap_both(value):
        pairs = [(r * parts + c, (r ^ 1) * parts + (c ^ 1)) for r in range(reps) for c in range(parts)]
        return lax.ppermute(value, ("rep", "ctx"), pairs)

    def last_sums(value):
        for axis, bit in last_steps[:-1]:
            (value,) = call(sum_kernel, [low_like(*value.shape)], (idx, value, swap(value, axis, bit)), name="more")
        return value, swap(value, *last_steps[-1])

    def step(name, number, after):
        run = functools.partial(call, after=after, name=f"{name}_{number}")
        keep, *got = sums[name]
        if number == 1:
            value, send = run(halve_kernel, [low_like(*keep.shape[1:])] * 2, (idx, keep, *got))
            sums[name] = value, swap(send, "ctx", 1)
        elif number == 2:
            (value,) = run(sum_kernel, [low_like(*keep.shape)], (idx, keep, *got))
            sums[name] = last_sums(value)
        elif number == 3 and name == "d":
            (value,) = run(sum_kernel, [low_like(*keep.shape)], (idx, keep, *got))
            sums[name] = value, swap(value, "ctx", 1)
        elif name != "d" and number == 3:
            outs = [low_like(rows // 4, keep.shape[1])] * shards
            if name == "q":
                outs += [low_like(rows // 3, keep.shape[1]), full_like(EXTRA, keep.shape[1])]
            outs = list(run(functools.partial(deal_kernel, shards), outs, (idx, keep, *got)))
            value = outs[0]
            sums[name] = [value] + [swap(outs[bit], "fsdp", bit) for bit in range(1, shards)] + outs[shards : shards + 1]
            if name == "q":
                val["lines"] = outs[shards + 1]
        elif name != "d" and number == 4:
            blocks = sums[name]
            total_rows = sum(part.shape[0] for part in blocks)
            (value,) = run(
                functools.partial(join_kernel, shards), [low_like(total_rows, keep.shape[1])], (idx, *blocks)
            )
            if name == "q":
                sums[name] = value, swap(value, "rep", 1), swap(value, "ctx", 1), swap_both(value)
            else:
                sums[name] = value, swap(value, "ctx", 1)
        else:
            (value,) = run(stack_kernel, [low_like(2, *keep.shape)], (idx, keep, *got))
            sums[name] = value, swap(value, "rep", 1)
        return value

    qkv_places = tuple(
        tuple((s * rows, (s + 1) * rows, s * width + f * rows) for s in range(3)) for f in range(shards)
    )
    val = {}
    cut = lambda full: lax.dynamic_slice_in_dim(full, own * rows, rows, 1)
    shared = [full_like(2 * seg, width), low_like(2 * seg, width)]

    def run_unit_grads(after):
        down_keep, down_send, up_keep, up_send, val["cot_sum"] = call(
            unit_grads_kernel,
            [low_like(2, padded // 4, width)] * 2 + [low_like(2, rows, units)] * 2 + [full_like(1, width)],
            (idx, activated, cot, normed_two, hidden_grad),
            [pltpu.VMEM((padded, width), F32), pltpu.VMEM((width, units), F32)],
            name="unit_grads",
        us=8,
            after=after,
        )
        sums["d"] = down_keep, swap(down_send, "rep", 1)
        sums["u"] = up_keep, swap(up_send, "rep", 1)
        return val["cot_sum"]

    def run_norm_two_grad(after):
        keep, send = call(
            norm_grad_kernel,
            shared,
            (idx, hidden_grad, up_own),
            [pltpu.VMEM((total, width), F32)],
            name="norm_two_grad",
        us=4,
            after=after,
        )
        val["two"] = keep, swap(send, "fsdp", 1)
        return keep

    def run_branch(after):
        keep, send = call(
            branch_kernel,
            shared,
            (idx, activated, down_weight),
            [pltpu.VMEM((total, width), F32)],
            name="branch",
        us=4,
            after=after,
        )
        val["out"] = keep, swap(send, "fsdp", 1)
        return keep

    def run_add(key, after):
        near, onward = call(
            add_kernel,
            [full_like(seg, width), low_like(seg, width)],
            (idx, *val[key]),
            name="add_" + key,
            after=after,
        )
        val[key] = near, swap(onward, "fsdp", 2)
        return near

    def run_norm_two_back(after):
        val["attended_grad"], low_grad, val["sums_two"] = call(
            functools.partial(norm_back_kernel, 2),
            [full_like(seg, width), low_like(seg, width), full_like(2, width)],
            (idx, *val["two"], attended_own, cot_own, vectors),
            name="norm_two_back",
            after=after,
        )
        val["branch_grad"] = gather(low_grad)
        return val["sums_two"]

    def run_attend_back(after):
        val["branch_grad"], val["projected_grad"], val["sum_q"], val["sum_v"], val["branch_sum"] = call(
            attend_back_kernel,
            [
                low_like(total, width),
                low_like(total, 3 * rows),
                full_like(1, rows),
                full_like(1, rows),
                full_like(1, width),
            ],
            (idx, *val["branch_grad"], out_weight, pic_col, pic_row, queries, keys, values, logs),
            [pltpu.VMEM((total, rows), BF)],
            name="attend_back",
        us=9,
            after=after,
        )
        return val["sum_q"]

    def run_qkv_grads(after):
        names = ("sum_q", "sum_v", "branch_sum", "cot_sum")
        keep, send = call(
            qkv_grads_kernel,
            [low_like(2, rows + rows // 3 + EXTRA, 3 * rows)] * 2,
            (
                idx, normed_one, val["projected_grad"], mixed, val["branch_grad"], *(val[name] for name in names),
                up_bias_grad, val["sums_one"], val["sums_two"],
            ),
            [pltpu.VMEM((width, 3 * rows), F32), pltpu.VMEM((rows, width), F32), pltpu.VMEM((EXTRA, 3 * rows), F32)],
            name="qkv_grads",
        us=5,
            after=after,
        )
        sums["q"] = keep, swap(send, "rep", 1)
        return keep

    def run_norm_one_grad(after):
        keep, send, val["sums_one"] = call(
            norm_grad_sums_kernel,
            shared + [full_like(2, width)],
            (idx, val["projected_grad"], qkv_own, tokens),
            [pltpu.VMEM((total, width), F32)],
            name="norm_one_grad",
        us=4,
            after=after,
        )
        val["one"] = keep, swap(send, "fsdp", 1)
        return keep

    def run_norm_one_back(after):
        low_grad, _ = call(
            functools.partial(norm_back_kernel, 0),
            [low_like(seg, width), full_like(2, width)],
            (idx, *val["one"], tokens_own, val["attended_grad"], vectors),
            name="norm_one_back",
            after=after,
        )
        val["input_grad"] = low_grad
        return low_grad

    def run_output(after):
        (low,) = call(
            output_kernel, [low_like(seg, width)], (idx, *val["out"], attended_own, vectors), name="output", after=after
        )
        val["output"] = low
        return low

    def run_lines(number, after):
        if number > 1:
            (val["lines"],) = call(
                total_kernel,
                [full_like(*val["lines"].shape)],
                (idx, *val["lines_parts"]),
                name=f"lines_{number}",
                after=after,
            )
        else:
            val["own_lines"] = val["lines"]
        if number < 3:
            val["lines_parts"] = val["lines"], swap(val["lines"], "fsdp", number)
        return val["lines"]

    def run_share_back(after):
        val["shared"] = share_back(val["output"], val["input_grad"])
        return after[0]

    def run_outputs(after):
        outs = call(
            part_tokens_kernel, [low_like(shards, piece, width)] * 2, (idx, val["shared"]), name="outs", after=after
        )
        val["output"], val["input_grad"] = (value.reshape(seg, width) for value in outs)
        return outs[0]

    def run_place(key, after):
        run = functools.partial(call, name="place_" + key, after=after)
        if key == "d":
            (val["d"],) = run(place_down_kernel, [full_like(units, width)], (idx, *sums["d"]))
        elif key == "u":
            (val["u"],) = run(place_up_kernel, [full_like(rows, shards * units)], (idx, *sums["u"]))
        else:
            outs = [full_like(rows, 3 * width), full_like(rows, width)]
            val["q"], val["o"] = run(functools.partial(place_qkv_kernel, qkv_places), outs, (idx, *sums["q"]))
        return val[key]

    tasks = {
        "ugrads": run_unit_grads,
        "ng2": run_norm_two_grad,
        "br": run_branch,
        "add2": functools.partial(run_add, "two"),
        "addo": functools.partial(run_add, "out"),
        "add1": functools.partial(run_add, "one"),
        "K3": run_norm_two_back,
        "K4": run_attend_back,
        "K5": run_norm_one_back,
        "fin": run_output,
        "back": run_share_back,
        "outs": run_outputs,
        "qg": run_qkv_grads,
        "ng1": run_norm_one_grad,
    }
    token = (hidden_grad,)
    for name in SCHEDULE:
        if name in tasks:
            token = (tasks[name](token),)
        elif name.startswith("place_"):
            token = (run_place(name[6:], token),)
        elif name.startswith("v"):
            token = (run_lines(int(name[1:]), token),)
        else:
            token = (step(name[:-1], int(name[-1]), token),)
    lines, own_lines = val["lines"], val["own_lines"]
    vector_of = lambda i: own_lines[i // 3, i % 3 * rows : (i % 3 + 1) * rows]
    norms = jnp.concatenate([lines[4:12:2], lines[5:12:2, :rows]], axis=1)
    norms = lax.dynamic_slice_in_dim(norms, own * rows, rows, 1)
    return (
        val["output"][None],
        val["input_grad"][None],
        norms[0],
        norms[1],
        val["q"],
        vector_of(0),
        vector_of(1),
        val["o"],
        vector_of(2),
        norms[2],
        norms[3],
        val["u"],
        own_lines[2:4].reshape(-1)[:units],
        val["d"],
        vector_of(3),
    )


def solution(mesh):
    sizes = tuple(mesh.shape[axis] for axis in ("rep", "fsdp", "ctx"))
    tokens = P(("rep", "fsdp"), "ctx", None)
    vector, matrix = P("fsdp"), P("fsdp", None)
    return jax.shard_map(
        functools.partial(per_device, sizes),
        mesh=mesh,
        in_specs=(
            tokens,
            P(("rep", "fsdp"), None),
            vector,
            vector,
            matrix,
            vector,
            vector,
            matrix,
            vector,
            vector,
            vector,
            matrix,
            vector,
            matrix,
            vector,
            tokens,
        ),
        out_specs=(
            tokens,
            tokens,
            vector,
            vector,
            matrix,
            vector,
            vector,
            matrix,
            vector,
            vector,
            vector,
            matrix,
            vector,
            matrix,
            vector,
        ),
        check_vma=False,
    )
```
